512 devices in a mesh: ax: 16 (over y_hi, x, core), xs: 32 (over y_lo, z).
Axes of the slice: x: 4, y: 4 (y_hi: 2, y_lo: 2; y = y_hi * 2 + y_lo), z: 16, core: 2. Of those that a mesh axis runs over, the one named last changes fastest.
Arguments:
- concentrations_before: float32 [9, 192, 128, 1024], P(None, 'ax', 'xs'), may hold values from 0.05 to 1
- thermal_field_before: float32 [192, 128, 1024], P('ax', 'xs'), may hold values from 0.8 to 2.5
- flow_speed_vector: float32 [3, 192, 128, 1024], P(None, 'ax', 'xs'), may hold values from -4 to 4
- gap_indicator: int32 [192, 128, 1024], P('ax', 'xs'), may hold values 0 or 1
- destination_slice: int32 [192], replicated, may hold values from 0 to 191, as said below
- reaction_rate_constant: float32 [9], replicated, may hold values from 0.5 to 4
- threshold_kelvin: float32 [9], replicated, may hold values from 0.5 to 3
- reaction_coefficient_matrix: float32 [9, 9], replicated, may hold values from -2 to 2
- energy_release: float32 [9], replicated, may hold values from -4 to 4
- viewer_picture: float32 [128, 1024], P('xs', 'ax'), may hold values from 0 to 1.5
Outputs:
- concentrations_after: float32 [9, 192, 128, 1024], P(None, 'ax', 'xs')
- thermal_field_after: float32 [192, 128, 1024], P('ax', 'xs')
- image_error: float32 [128, 1024], P('xs', 'ax')
The draws below stay inside these ranges and needn't reach their ends.
Inputs may be any that keep to these rules, and one draw needn't show every extreme that they name: destination_slice[p] = p minus the number of 2 distinct merge positions (each in 1 to 191) at or before p, one of which lies in 1 to 12; so destination_slice is nondecreasing, lies in [p - 2, p], and each new plane from 0 to 189 receives between one and 3 old planes (more than two only where merge positions are adjacent).
All inputs are finite; a program needn't handle non-finite values. No bound on the sum of `gap_indicator` on one device may be relied on, other than what follows from the above.
Results may differ from the reference program's by a relative error of at most 0.000053.
Values sent between devices are 32-bit elements; how exact they have to be, the bound alone decides.
A program may use at most 64 MiB of HBM per device.

```python
import math
import jax
import jax.numpy as jnp
from jax import lax

SPECIES_TOTAL = 9
CA = 12
MESH_ROWS_OUTER = 1024
LENGTHWISE_SLICES = 192
MESH_ROWS_INNER = 128


def draw_destination_slice(key, part):
    first_key = jax.random.fold_in(key, 11)
    order_key = jax.random.fold_in(key, 23)
    early = jax.random.randint(first_key, (), 1, CA + 1).astype(jnp.int32)
    order = (jax.random.permutation(order_key, LENGTHWISE_SLICES - 1) + 1).astype(jnp.int32)
    second = jnp.where(order[0] == early, order[1], order[0]).astype(jnp.int32)
    picks = jnp.stack([early, second])
    planes = jnp.arange(LENGTHWISE_SLICES, dtype=jnp.int32)
    merged = jnp.sum((picks[:, None] <= planes[None, :]).astype(jnp.int32), axis=0)
    return (planes - merged).astype(jnp.int32)


def plant(result, stream_key, smallest, high):
    extent = result.shape
    index_at = [jax.random.randint(jax.random.fold_in(stream_key, axis), (), 0, extent[axis]) for axis in range(len(extent))]
    result = result.at[tuple(index_at)].set(smallest)
    longest = extent.index(max(extent))
    index_at[longest] = (index_at[longest] + 1) % extent[longest]
    return result.at[tuple(index_at)].set(high)


def steps_of(own_key, dims, shards, low, high):
    gain = 1.0
    for position, blocks in shards:
        heights = jax.random.uniform(jax.random.fold_in(jax.random.fold_in(own_key, 6), position), (blocks,), jnp.float32, low / len(shards), high / len(shards))
        gain = gain * jnp.repeat(jnp.exp(heights), dims[position] // blocks).reshape((-1,) + (1,) * (len(dims) - 1 - position))
    return gain


def normal_values(stream_key, shape, deviation, reach, shards=(), held_as=jnp.bfloat16):
    values = deviation * jax.random.normal(stream_key, shape, jnp.float32)
    if shards:
        values = values * steps_of(stream_key, shape, shards, -0.22, 0.18)
    return jnp.clip(values, -reach, reach).astype(held_as)


def setup_inputs(seed: int = 0) -> dict:
    seeds = jax.random.split(jax.random.key(seed), 11)
    concentrations_before = jnp.clip(0.05 + 0.95 * jax.random.uniform(seeds[0], (SPECIES_TOTAL, LENGTHWISE_SLICES, MESH_ROWS_INNER, MESH_ROWS_OUTER), jnp.float32) ** steps_of(seeds[0], (SPECIES_TOTAL, LENGTHWISE_SLICES, MESH_ROWS_INNER, MESH_ROWS_OUTER), ((1, 16), (2, 32)), -0.2, 0.2), 0.05, 1.0)
    thermal_field_before = jnp.clip(0.8 + 1.7 * jax.random.uniform(seeds[1], (LENGTHWISE_SLICES, MESH_ROWS_INNER, MESH_ROWS_OUTER), jnp.float32) ** steps_of(seeds[1], (LENGTHWISE_SLICES, MESH_ROWS_INNER, MESH_ROWS_OUTER), ((0, 16), (1, 32)), -0.2, 0.2), 0.8, 2.5)
    flow_speed_vector = normal_values(seeds[2], (3, LENGTHWISE_SLICES, MESH_ROWS_INNER, MESH_ROWS_OUTER), 1.0, 4.0, ((1, 16), (2, 32)), jnp.float32)
    gap_indicator = plant((jax.random.randint(seeds[3], (LENGTHWISE_SLICES, MESH_ROWS_INNER, MESH_ROWS_OUTER), 0, 4) < 1).astype(jnp.int32), jax.random.fold_in(seeds[3], 1), 0, 1)
    destination_slice = draw_destination_slice(jax.random.fold_in(seeds[10], 71), 0)
    reaction_rate_constant = jnp.clip(jnp.exp(jax.random.uniform(seeds[5], (SPECIES_TOTAL,), jnp.float32, math.log(0.5), math.log(4.0))), 0.5, 4.0)
    threshold_kelvin = jnp.clip(jnp.exp(jax.random.uniform(seeds[6], (SPECIES_TOTAL,), jnp.float32, math.log(0.5), math.log(3.0))), 0.5, 3.0)
    reaction_coefficient_matrix = normal_values(seeds[7], (SPECIES_TOTAL, SPECIES_TOTAL), SPECIES_TOTAL ** -0.5, 2.0, (), jnp.float32)
    energy_release = normal_values(seeds[8], (SPECIES_TOTAL,), 1.0, 4.0, (), jnp.float32)
    viewer_picture = jnp.clip(1.5 * jax.random.uniform(seeds[9], (MESH_ROWS_INNER, MESH_ROWS_OUTER), jnp.float32) ** steps_of(seeds[9], (MESH_ROWS_INNER, MESH_ROWS_OUTER), ((0, 32), (1, 16)), -0.2, 0.2), 0.0, 1.5)
    return {"concentrations_before": concentrations_before, "thermal_field_before": thermal_field_before, "flow_speed_vector": flow_speed_vector, "gap_indicator": gap_indicator, "destination_slice": destination_slice, "reaction_rate_constant": reaction_rate_constant, "threshold_kelvin": threshold_kelvin, "reaction_coefficient_matrix": reaction_coefficient_matrix, "energy_release": energy_release, "viewer_picture": viewer_picture}


def remap_planes(extended, owner_part, first, count_new, fallback):
    targets = first + jnp.arange(count_new, dtype=jnp.int32)
    onehot = (owner_part[None, :] == targets[:, None]).astype(jnp.float32)
    summed = jnp.einsum("qp,cpyz->cqyz", onehot, extended, precision=lax.Precision.HIGHEST)
    counts = jnp.sum(onehot, axis=1)
    scaled = summed / jnp.maximum(counts, 1.0)[None, :, None, None]
    return jnp.where((counts > 0.0)[None, :, None, None], scaled, fallback)


def chemistry(center, reaction_rate_constant, threshold_kelvin, reaction_coefficient_matrix, energy_release):
    ys = center[:SPECIES_TOTAL]
    temp = center[SPECIES_TOTAL]
    rates = reaction_rate_constant[:, None, None, None] * jnp.exp(-threshold_kelvin[:, None, None, None] / temp[None]) * ys * jnp.roll(ys, -1, axis=0)
    source = jnp.einsum("sr,ryz->syz", reaction_coefficient_matrix, rates.reshape(SPECIES_TOTAL, rates.shape[1], -1), precision=lax.Precision.HIGHEST).reshape(rates.shape)
    warming_source = jnp.einsum("r,ryz->yz", energy_release, rates.reshape(SPECIES_TOTAL, rates.shape[1], -1), precision=lax.Precision.HIGHEST).reshape(rates.shape[1:])
    return source, warming_source


def reference(concentrations_before, thermal_field_before, flow_speed_vector, gap_indicator, destination_slice, reaction_rate_constant, threshold_kelvin, reaction_coefficient_matrix, energy_release, viewer_picture):
    earlier_fields = jnp.concatenate([concentrations_before, thermal_field_before[None]], axis=0)
    remapped = remap_planes(earlier_fields, destination_slice, jnp.int32(0), LENGTHWISE_SLICES, earlier_fields)
    padded = jnp.pad(remapped, ((0, 0), (1, 1), (1, 1), (1, 1)))
    upper_a = padded[:, 2:, 1:-1, 1:-1]
    lower_a = padded[:, :-2, 1:-1, 1:-1]
    upper_y = padded[:, 1:-1, 2:, 1:-1]
    lower_y = padded[:, 1:-1, :-2, 1:-1]
    upper_z = padded[:, 1:-1, 1:-1, 2:]
    lower_z = padded[:, 1:-1, 1:-1, :-2]
    lap = upper_a + lower_a + upper_y + lower_y + upper_z + lower_z - 6.0 * remapped
    adv = 0.5 * (flow_speed_vector[0][None] * (upper_a - lower_a) + flow_speed_vector[1][None] * (upper_y - lower_y) + flow_speed_vector[2][None] * (upper_z - lower_z))
    advective_current = remapped + 0.1 * lap - 0.2 * adv
    source, warming_source = chemistry(remapped, reaction_rate_constant, threshold_kelvin, reaction_coefficient_matrix, energy_release)
    fluid_blend = (1 - gap_indicator).astype(jnp.float32)
    concentrations_after = advective_current[:SPECIES_TOTAL] + 0.5 * fluid_blend[None] * source
    thermal_field_after = advective_current[SPECIES_TOTAL] + 0.5 * fluid_blend * warming_source
    glow_picture = jnp.sum(fluid_blend * concentrations_after[4] * thermal_field_after, axis=0) / LENGTHWISE_SLICES
    return concentrations_after, thermal_field_after, glow_picture - viewer_picture
```

```python
import functools

import jax
import jax.numpy as jnp
from jax import lax
from jax.experimental import pallas as pl
from jax.experimental.pallas import tpu as pltpu
from jax.sharding import PartitionSpec as P

SPECIES = 9
FIELDS = 10
ORDER = (9, 4, 0, 1, 2, 3, 5, 6, 7, 8)
PLACE = tuple(ORDER.index(f) for f in range(FIELDS))
GROUPS = ((0, 2), (2, 4), (6, 4))
ROWS = 4
LANES = 128
CHUNKS = 8
MESH = pl.DeviceIdType.MESH


def per_device_kernel(
    n_ax, n_xs, planes, total_planes,
    conc, temp, vel, gap, dest, rate_k, thresh, coeff, heat, picture,
    conc_out, temp_out, image_out,
    old, rem, vel_v, gap_v, coef, edge, gas, mix, img, img_in,
    load_sem, small_sem, ax_send, ax_recv, xs_send, xs_recv, img_send, img_recv,
    dest_s, rate_s, thresh_s, coeff_s, heat_s, picture_v,
):
    ax = lax.axis_index("ax")
    xs = lax.axis_index("xs")
    start = ax * planes

    barrier = pltpu.get_barrier_semaphore()
    for d in range(1, n_ax):
        pl.semaphore_signal(
            barrier, inc=1, device_id=(lax.rem(ax + d, n_ax), xs), device_id_type=MESH
        )
    for d in (1, n_xs - 1):
        pl.semaphore_signal(
            barrier, inc=1, device_id=(ax, lax.rem(xs + d, n_xs)), device_id_type=MESH
        )

    def local(src, dst, sem):
        copy = pltpu.make_async_copy(src, dst, sem)
        copy.start()
        return copy

    smalls = [
        local(dest, dest_s, small_sem.at[0]),
        local(rate_k, rate_s, small_sem.at[1]),
        local(thresh, thresh_s, small_sem.at[2]),
        local(coeff, coeff_s, small_sem.at[3]),
        local(heat, heat_s, small_sem.at[4]),
        local(picture, picture_v, small_sem.at[5]),
    ]
    own = pl.ds(1, planes)
    loads = [
        local(temp, old.at[0, own], load_sem.at[0]),
        local(conc.at[4], old.at[1, own], load_sem.at[1]),
        local(conc.at[pl.ds(0, 4)], old.at[pl.ds(2, 4), own], load_sem.at[2]),
        local(conc.at[pl.ds(5, 4)], old.at[pl.ds(6, 4), own], load_sem.at[3]),
        local(vel, vel_v, load_sem.at[4]),
        local(gap, gap_v, load_sem.at[5]),
    ]

    @pl.when(ax == 0)
    def _():
        old[:, 0] = jnp.zeros((FIELDS, 32, LANES), jnp.float32)

    @pl.when(ax == n_ax - 1)
    def _():
        old[:, pl.ds(planes + 1, 3)] = jnp.zeros((FIELDS, 3, 32, LANES), jnp.float32)

    img[...] = jnp.zeros_like(img)

    def row(r):
        return pl.ds(r, CHUNKS, stride=ROWS)

    def weights(q):
        new = start + q

        def hit(k):
            p = jnp.clip(new + k, 0, total_planes - 1)
            good = (dest_s[p] == new) & (new + k < total_planes) & (new + k >= 0)
            return good.astype(jnp.int32)

        h = [hit(k) for k in range(3)]
        count = h[0] + h[1] + h[2]
        inv = jnp.where(count == 3, 1.0 / 3.0, jnp.where(count == 2, 0.5, 1.0)).astype(
            jnp.float32
        )
        inside = ((new >= 0) & (new < total_planes)).astype(jnp.int32)
        none = (count == 0).astype(jnp.int32) * inside
        first = (h[0] + none).astype(jnp.float32) * inv
        return first, h[1].astype(jnp.float32) * inv, h[2].astype(jnp.float32) * inv

    def remap(first_field, fields, q0, count):
        def body(i, carry):
            q = q0 + i
            w = weights(q)
            for f in range(first_field, first_field + fields):
                for r in range(ROWS):
                    rem[f, q + 1, r + 1] = (
                        w[0] * old[f, q + 1, row(r), :]
                        + w[1] * old[f, q + 2, row(r), :]
                        + w[2] * old[f, q + 3, row(r), :]
                    )
            return carry

        lax.fori_loop(0, count, body, 0)

    def remap_low(first_field, fields):
        w = weights(-1)
        for f in range(first_field, first_field + fields):
            for r in range(ROWS):
                rem[f, 0, r + 1] = (
                    w[0] * old[f, 0, row(r), :]
                    + w[1] * old[f, 1, row(r), :]
                    + w[2] * old[f, 2, row(r), :]
                )

    down = (lax.max(ax - 1, 0), xs)
    up = (lax.min(ax + 1, n_ax - 1), xs)
    low3, top3 = pl.ds(0, 3), pl.ds(planes + 1, 3)
    ax_parts = (
        (lambda s: temp.at[s], (0,)),
        (lambda s: conc.at[4, s], (1,)),
        (lambda s: conc.at[pl.ds(0, 4), s], (pl.ds(2, 4),)),
        (lambda s: conc.at[pl.ds(5, 4), s], (pl.ds(6, 4),)),
    )

    def ax_copy(part, going_down):
        source, where = ax_parts[part]
        slot = 2 * part + (0 if going_down else 1)
        return pltpu.make_async_remote_copy(
            src_ref=source(low3 if going_down else planes - 1),
            dst_ref=old.at[where + ((top3 if going_down else 0),)],
            send_sem=ax_send.at[slot],
            recv_sem=ax_recv.at[slot],
            device_id=down if going_down else up,
            device_id_type=MESH,
        )

    spans = (pl.ds(1, planes - 2), pl.ds(planes - 1, 2))

    def xs_copy(group, span, going_down):
        f0, fn = GROUPS[group]
        slot = 4 * group + 2 * span + (0 if going_down else 1)
        fields = pl.ds(f0, fn)
        return pltpu.make_async_remote_copy(
            src_ref=rem.at[fields, spans[span], 1 if going_down else ROWS],
            dst_ref=rem.at[fields, spans[span], ROWS + 1 if going_down else 0],
            send_sem=xs_send.at[slot],
            recv_sem=xs_recv.at[slot],
            device_id=(ax, lax.max(xs - 1, 0) if going_down else lax.min(xs + 1, n_xs - 1)),
            device_id_type=MESH,
        )

    def xs_start(group, span):
        @pl.when(xs > 0)
        def _():
            xs_copy(group, span, True).start()

        @pl.when(xs < n_xs - 1)
        def _():
            xs_copy(group, span, False).start()

    smalls[0].wait()
    loads[0].wait()
    loads[1].wait()
    remap(0, 2, 0, planes - 2)
    pl.semaphore_wait(barrier, n_ax + 1)

    for part in range(4):
        @pl.when(ax > 0)
        def _():
            ax_copy(part, True).start()

        @pl.when(ax < n_ax - 1)
        def _():
            ax_copy(part, False).start()

    xs_start(0, 0)
    loads[2].wait()
    remap(2, 4, 0, planes - 2)
    xs_start(1, 0)
    loads[3].wait()
    remap(6, 4, 0, planes - 2)
    xs_start(2, 0)
    for small in smalls[1:]:
        small.wait()
    loads[4].wait()
    loads[5].wait()

    for s in range(SPECIES):
        for r in range(SPECIES):
            mix[s * SPECIES + r] = coeff_s[s, r] * rate_s[r]
    for r in range(SPECIES):
        mix[SPECIES * SPECIES + r] = heat_s[r] * rate_s[r]

    lane = lax.broadcasted_iota(jnp.int32, (CHUNKS, LANES), 1)
    chunk = lax.broadcasted_iota(jnp.int32, (CHUNKS, LANES), 0)
    at_last = lane == LANES - 1
    at_first = lane == 0
    z_end = at_last & (chunk == CHUNKS - 1)
    z_begin = at_first & (chunk == 0)

    def out_ref(i):
        f = ORDER[i]
        return temp_out if f == SPECIES else conc_out.at[f]

    def plane(q):
        for r in range(ROWS):
            for d in range(3):
                v = 0.1 * vel_v[d, q, row(r), :]
                above = 0.1 - v
                below = 0.1 + v
                if d == 2:
                    above = jnp.where(z_end, 0.0, above)
                    below = jnp.where(z_begin, 0.0, below)
                if d == 1 and r == 0:
                    edge[q, 0] = below
                if d == 1 and r == ROWS - 1:
                    edge[q, 1] = above
                coef[2 * d, r] = above
                coef[2 * d + 1, r] = below
            gas[q, r] = 0.5 * (1 - gap_v[q, row(r), :]).astype(jnp.float32)
        rates = []
        for r in range(ROWS):
            inv = -1.0 / rem[0, q + 1, r + 1]
            ys = [rem[PLACE[s], q + 1, r + 1] for s in range(SPECIES)]
            rates.append(
                [
                    jnp.exp(thresh_s[s] * inv) * (ys[s] * ys[(s + 1) % SPECIES])
                    for s in range(SPECIES)
                ]
            )
        for i in range(FIELDS):
            f = ORDER[i]
            source = [None] * ROWS
            for s in range(SPECIES):
                m = mix[f * SPECIES + s]
                for r in range(ROWS):
                    term = m * rates[r][s]
                    source[r] = term if source[r] is None else source[r] + term
            mine = [rem[i, q + 1, r + 1] for r in range(ROWS)]
            for r in range(ROWS):
                x = mine[r]
                to_up = pltpu.roll(x, LANES - 1, 1)
                to_up = jnp.where(at_last, pltpu.roll(to_up, CHUNKS - 1, 0), to_up)
                to_low = pltpu.roll(x, 1, 1)
                to_low = jnp.where(at_first, pltpu.roll(to_low, 1, 0), to_low)
                total = 0.4 * x + gas[q, r] * source[r]
                total += coef[0, r] * rem[i, q + 2, r + 1] + coef[1, r] * rem[i, q, r + 1]
                total += coef[4, r] * to_up + coef[5, r] * to_low
                if r > 0:
                    total += coef[3, r] * mine[r - 1]
                if r < ROWS - 1:
                    total += coef[2, r] * mine[r + 1]
                out_ref(i)[q, row(r), :] = total

    def run_planes(first, count):
        def body(i, carry):
            plane(first + i)
            return carry

        lax.fori_loop(0, count, body, 0)

    run_planes(1, planes - 4)

    for group, parts in enumerate(((0, 1), (2,), (3,))):
        for part in parts:
            @pl.when(ax < n_ax - 1)
            def _():
                ax_copy(part, True).wait_recv()

            @pl.when(ax > 0)
            def _():
                ax_copy(part, False).wait_recv()
        f0, fn = GROUPS[group]
        remap(f0, fn, planes - 2, 3)
        xs_start(group, 1)
        remap_low(f0, fn)

    run_planes(0, 1)
    run_planes(planes - 3, 3)

    def add_rows(group):
        f0, fn = GROUPS[group]

        def side(is_low):
            r = 0 if is_low else ROWS - 1
            halo = 0 if is_low else ROWS + 1

            def body(q, carry):
                c = edge[q, 0 if is_low else 1]
                for i in range(f0, f0 + fn):
                    ref = out_ref(i)
                    ref[q, row(r), :] = ref[q, row(r), :] + c * rem[i, q + 1, halo]
                return carry

            for span in range(2):
                xs_copy(group, span, not is_low).wait_recv()
            lax.fori_loop(0, planes, body, 0)

        @pl.when(xs > 0)
        def _():
            side(True)

        @pl.when(xs < n_xs - 1)
        def _():
            side(False)

    add_rows(0)

    def glow(q, sums):
        return tuple(
            sums[r]
            + gas[q, r] * out_ref(1)[q, row(r), :] * out_ref(0)[q, row(r), :]
            for r in range(ROWS)
        )

    zero = jnp.zeros((CHUNKS, LANES), jnp.float32)
    sums = lax.fori_loop(0, planes, glow, (zero,) * ROWS)
    for r in range(ROWS):
        img[pl.ds(r, CHUNKS, stride=CHUNKS), :] = sums[r]

    def img_copy(d):
        peer = lax.rem(ax + d, n_ax)
        tile = pl.ds(pl.multiple_of((peer // 2) * CHUNKS, CHUNKS), CHUNKS)
        return pltpu.make_async_remote_copy(
            src_ref=img.at[tile],
            dst_ref=img_in.at[d - 1],
            send_sem=img_send.at[d - 1],
            recv_sem=img_recv.at[d - 1],
            device_id=(peer, xs),
            device_id_type=MESH,
        )

    for d in range(1, n_ax):
        img_copy(d).start()

    add_rows(1)
    add_rows(2)

    mine = img[pl.ds(pl.multiple_of((ax // 2) * CHUNKS, CHUNKS), CHUNKS), :]
    for d in range(1, n_ax):
        img_copy(d).wait_recv()
        mine = mine + img_in[d - 1]
    half = LANES // 2
    mine = jnp.where(lax.rem(ax, 2) == 1, pltpu.roll(mine, half, 1), mine)
    image_out[...] = mine[:ROWS, :half] * (2.0 / total_planes) - picture_v[...]

    for d in range(1, n_ax):
        img_copy(d).wait_send()
    for part in range(4):
        @pl.when(ax > 0)
        def _():
            ax_copy(part, True).wait_send()

        @pl.when(ax < n_ax - 1)
        def _():
            ax_copy(part, False).wait_send()
    for group in range(3):
        for span in range(2):
            @pl.when(xs > 0)
            def _():
                xs_copy(group, span, True).wait_send()

            @pl.when(xs < n_xs - 1)
            def _():
                xs_copy(group, span, False).wait_send()


def tiled(x):
    *lead, rows, width = x.shape
    x = x.reshape(*lead, rows, width // LANES, LANES)
    return jnp.swapaxes(x, -3, -2).reshape(*lead, rows * (width // LANES), LANES)


def untiled(x, rows):
    *lead, both, lanes = x.shape
    x = x.reshape(*lead, both // rows, rows, lanes)
    return jnp.swapaxes(x, -3, -2).reshape(*lead, rows, (both // rows) * lanes)


def solution(mesh):
    n_ax, n_xs = mesh.shape["ax"], mesh.shape["xs"]

    def per_device(conc, temp, vel, gap, dest, rate_k, thresh, coeff, heat, picture):
        planes = conc.shape[1]
        total_planes = planes * n_ax
        f32 = jnp.float32
        any_space = pl.BlockSpec(memory_space=pltpu.HBM)
        vmem = pl.BlockSpec(memory_space=pltpu.VMEM)
        dma = pltpu.SemaphoreType.DMA
        both = ROWS * CHUNKS
        c, t, image = pl.pallas_call(
            functools.partial(per_device_kernel, n_ax, n_xs, planes, total_planes),
            out_shape=(
                jax.ShapeDtypeStruct((SPECIES, planes, both, LANES), f32),
                jax.ShapeDtypeStruct((planes, both, LANES), f32),
                jax.ShapeDtypeStruct(picture.shape, f32),
            ),
            in_specs=[any_space] * 10,
            out_specs=(vmem, vmem, vmem),
            scratch_shapes=[
                pltpu.VMEM((FIELDS, planes + 4, both, LANES), f32),
                pltpu.VMEM((FIELDS, planes + 2, ROWS + 2, CHUNKS, LANES), f32),
                pltpu.VMEM((3, planes, both, LANES), f32),
                pltpu.VMEM((planes, both, LANES), jnp.int32),
                pltpu.VMEM((6, ROWS, CHUNKS, LANES), f32),
                pltpu.VMEM((planes, 2, CHUNKS, LANES), f32),
                pltpu.VMEM((planes, ROWS, CHUNKS, LANES), f32),
                pltpu.SMEM((FIELDS * SPECIES,), f32),
                pltpu.VMEM((CHUNKS * CHUNKS, LANES), f32),
                pltpu.VMEM((n_ax - 1, CHUNKS, LANES), f32),
                dma((6,)),
                dma((6,)),
                dma((8,)),
                dma((8,)),
                dma((12,)),
                dma((12,)),
                dma((n_ax - 1,)),
                dma((n_ax - 1,)),
                pltpu.SMEM(dest.shape, jnp.int32),
                pltpu.SMEM(rate_k.shape, f32),
                pltpu.SMEM(thresh.shape, f32),
                pltpu.SMEM(coeff.shape, f32),
                pltpu.SMEM(heat.shape, f32),
                pltpu.VMEM(picture.shape, f32),
            ],
            compiler_params=pltpu.CompilerParams(
                collective_id=0, has_side_effects=True, vmem_limit_bytes=24 * 1024 * 1024
            ),
            name="fused_step",
        )(
            *(
                pltpu.with_memory_space_constraint(x, pltpu.HBM)
                for x in (
                    tiled(conc), tiled(temp), tiled(vel), tiled(gap),
                    dest, rate_k, thresh, coeff, heat, picture,
                )
            )
        )
        return untiled(c, ROWS), untiled(t, ROWS), image

    in_specs = (
        P(None, "ax", "xs", None),
        P("ax", "xs", None),
        P(None, "ax", "xs", None),
        P("ax", "xs", None),
        P(),
        P(),
        P(),
        P(),
        P(),
        P("xs", "ax"),
    )
    out_specs = (P(None, "ax", "xs", None), P("ax", "xs", None), P("xs", "ax"))
    return jax.shard_map(
        per_device, mesh=mesh, in_specs=in_specs, out_specs=out_specs, check_vma=False
    )
```

```python
import functools

import jax
import jax.numpy as jnp
from jax import lax
from jax.experimental import pallas as pl
from jax.experimental.pallas import tpu as pltpu
from jax.sharding import PartitionSpec as P

SPECIES = 9
FIELDS = 10
ORDER = (9, 4, 0, 1, 2, 3, 5, 6, 7, 8)
PLACE = tuple(ORDER.index(f) for f in range(FIELDS))
GROUPS = ((0, 2), (2, 4), (6, 4))
ROWS = 4
LANES = 128
CHUNKS = 8
MESH = pl.DeviceIdType.MESH


def per_device_kernel(
    n_ax, n_xs, planes, total_planes,
    conc, temp, vel, gap, dest, rate_k, thresh, coeff, heat, picture,
    conc_out, temp_out, image_out,
    old, rem, vel_v, gap_v, coef, edge, gas, mix, img, img_in,
    load_sem, small_sem, ax_send, ax_recv, xs_send, xs_recv, img_send, img_recv,
    known, dest_s, rate_s, thresh_s, coeff_s, heat_s, picture_v,
):
    ax = lax.axis_index("ax")
    xs = lax.axis_index("xs")
    start = ax * planes

    barrier = pltpu.get_barrier_semaphore()
    def greet(semaphore, distance):
        for d in (distance, n_ax - distance):
            pl.semaphore_signal(
                semaphore, inc=1, device_id=(lax.rem(ax + d, n_ax), xs), device_id_type=MESH
            )

    greet(barrier, 1)
    has_low, has_high = xs > 0, xs < n_xs - 1

    @pl.when(has_low)
    def _():
        pl.semaphore_signal(barrier, inc=1, device_id=(ax, xs - 1), device_id_type=MESH)

    @pl.when(has_high)
    def _():
        pl.semaphore_signal(barrier, inc=1, device_id=(ax, xs + 1), device_id_type=MESH)


    def local(src, dst, sem):
        copy = pltpu.make_async_copy(src, dst, sem)
        copy.start()
        return copy

    smalls = [
        local(dest, dest_s, small_sem.at[0]),
        local(rate_k, rate_s, small_sem.at[1]),
        local(thresh, thresh_s, small_sem.at[2]),
        local(coeff, coeff_s, small_sem.at[3]),
        local(heat, heat_s, small_sem.at[4]),
        local(picture, picture_v, small_sem.at[5]),
    ]
    own = pl.ds(1, planes)
    loads = [
        local(temp, old.at[0, own], load_sem.at[0]),
        local(conc.at[4], old.at[1, own], load_sem.at[1]),
        local(conc.at[pl.ds(0, 4)], old.at[pl.ds(2, 4), own], load_sem.at[2]),
        local(conc.at[pl.ds(5, 4)], old.at[pl.ds(6, 4), own], load_sem.at[3]),
        local(vel, vel_v, load_sem.at[4]),
        local(gap, gap_v, load_sem.at[5]),
    ]

    @pl.when(ax == 0)
    def _():
        old[:, 0] = jnp.zeros((FIELDS, 32, LANES), jnp.float32)

    @pl.when(ax == n_ax - 1)
    def _():
        old[:, pl.ds(planes + 1, 3)] = jnp.zeros((FIELDS, 3, 32, LANES), jnp.float32)

    img[...] = jnp.zeros_like(img)

    def row(r):
        return pl.ds(r, CHUNKS, stride=ROWS)

    def weights(q):
        new = start + q

        def hit(k):
            p = jnp.clip(new + k, 0, total_planes - 1)
            good = (dest_s[p] == new) & (new + k < total_planes) & (new + k >= 0)
            return good.astype(jnp.int32)

        h = [hit(k) for k in range(3)]
        count = h[0] + h[1] + h[2]
        inv = jnp.where(count == 3, 1.0 / 3.0, jnp.where(count == 2, 0.5, 1.0)).astype(
            jnp.float32
        )
        inside = ((new >= 0) & (new < total_planes)).astype(jnp.int32)
        none = (count == 0).astype(jnp.int32) * inside
        first = (h[0] + none).astype(jnp.float32) * inv
        return first, h[1].astype(jnp.float32) * inv, h[2].astype(jnp.float32) * inv

    def remap(first_field, fields, q0, count):
        def body(i, carry):
            q = q0 + i
            w = weights(q)
            for f in range(first_field, first_field + fields):
                for r in range(ROWS):
                    rem[f, q + 1, r + 1] = (
                        w[0] * old[f, q + 1, row(r), :]
                        + w[1] * old[f, q + 2, row(r), :]
                        + w[2] * old[f, q + 3, row(r), :]
                    )
            return carry

        lax.fori_loop(0, count, body, 0)

    def remap_low(first_field, fields):
        w = weights(-1)
        for f in range(first_field, first_field + fields):
            for r in range(ROWS):
                rem[f, 0, r + 1] = (
                    w[0] * old[f, 0, row(r), :]
                    + w[1] * old[f, 1, row(r), :]
                    + w[2] * old[f, 2, row(r), :]
                )

    down = (lax.max(ax - 1, 0), xs)
    up = (lax.min(ax + 1, n_ax - 1), xs)
    low3, top3 = pl.ds(0, 3), pl.ds(planes + 1, 3)
    low2, top2 = pl.ds(0, 2), pl.ds(planes + 1, 2)
    firsts, lasts = pl.ds(0, 4), pl.ds(2, 4)
    seconds, ends = pl.ds(5, 4), pl.ds(6, 4)
    down_parts = (
        (temp.at[low3], (0, top3)),
        (conc.at[4, low3], (1, top3)),
        (conc.at[firsts, low2], (lasts, top2)),
        (conc.at[seconds, low2], (ends, top2)),
        (conc.at[firsts, 2], (lasts, planes + 3)),
        (conc.at[seconds, 2], (ends, planes + 3)),
    )
    up_parts = (
        (temp.at[planes - 1], (0, 0)),
        (conc.at[4, planes - 1], (1, 0)),
        (conc.at[firsts, planes - 1], (lasts, 0)),
        (conc.at[seconds, planes - 1], (ends, 0)),
    )

    def ax_copy(part, going_down):
        source, where = (down_parts if going_down else up_parts)[part]
        slot = part + (0 if going_down else len(down_parts))
        return pltpu.make_async_remote_copy(
            src_ref=source,
            dst_ref=old.at[where],
            send_sem=ax_send.at[slot],
            recv_sem=ax_recv.at[slot],
            device_id=down if going_down else up,
            device_id_type=MESH,
        )

    def each_down(parts, sending, act):
        @pl.when(ax > 0 if sending else ax < n_ax - 1)
        def _():
            for part in parts:
                act(ax_copy(part, True))

    def each_up(parts, sending, act):
        @pl.when(ax < n_ax - 1 if sending else ax > 0)
        def _():
            for part in parts:
                act(ax_copy(part, False))

    spans = (pl.ds(1, planes - 2), pl.ds(planes - 1, 2))

    def xs_copy(group, span, going_down):
        f0, fn = GROUPS[group]
        slot = 4 * group + 2 * span + (0 if going_down else 1)
        fields = pl.ds(f0, fn)
        return pltpu.make_async_remote_copy(
            src_ref=rem.at[fields, spans[span], 1 if going_down else ROWS],
            dst_ref=rem.at[fields, spans[span], ROWS + 1 if going_down else 0],
            send_sem=xs_send.at[slot],
            recv_sem=xs_recv.at[slot],
            device_id=(ax, lax.max(xs - 1, 0) if going_down else lax.min(xs + 1, n_xs - 1)),
            device_id_type=MESH,
        )

    def xs_start(group, span):
        @pl.when(xs > 0)
        def _():
            xs_copy(group, span, True).start()

        @pl.when(xs < n_xs - 1)
        def _():
            xs_copy(group, span, False).start()

    smalls[0].wait()
    loads[0].wait()
    loads[1].wait()
    remap(0, 2, 0, planes - 2)
    loads[2].wait()
    remap(2, 4, 0, planes - 2)
    loads[3].wait()
    remap(6, 4, 0, planes - 2)
    pl.semaphore_wait(barrier, 2 + has_low.astype(jnp.int32) + has_high.astype(jnp.int32))

    each_down(range(2), True, lambda c: c.start())
    xs_start(0, 0)
    each_down(range(2, 6), True, lambda c: c.start())
    each_up(range(4), True, lambda c: c.start())
    xs_start(1, 0)
    greet(known.at[0], 1)
    for small in smalls[1:]:
        small.wait()
    loads[4].wait()
    loads[5].wait()

    for s in range(SPECIES):
        for r in range(SPECIES):
            mix[s * SPECIES + r] = coeff_s[s, r] * rate_s[r]
    for r in range(SPECIES):
        mix[SPECIES * SPECIES + r] = heat_s[r] * rate_s[r]

    lane = lax.broadcasted_iota(jnp.int32, (CHUNKS, LANES), 1)
    chunk = lax.broadcasted_iota(jnp.int32, (CHUNKS, LANES), 0)
    at_last = lane == LANES - 1
    at_first = lane == 0
    z_end = at_last & (chunk == CHUNKS - 1)
    z_begin = at_first & (chunk == 0)

    def out_ref(i):
        f = ORDER[i]
        return temp_out if f == SPECIES else conc_out.at[f]

    def plane(q):
        for r in range(ROWS):
            for d in range(3):
                v = 0.1 * vel_v[d, q, row(r), :]
                above = 0.1 - v
                below = 0.1 + v
                if d == 2:
                    above = jnp.where(z_end, 0.0, above)
                    below = jnp.where(z_begin, 0.0, below)
                if d == 1 and r == 0:
                    edge[q, 0] = below
                if d == 1 and r == ROWS - 1:
                    edge[q, 1] = above
                coef[2 * d, r] = above
                coef[2 * d + 1, r] = below
            gas[q, r] = 0.5 * (1 - gap_v[q, row(r), :]).astype(jnp.float32)
        rates = []
        for r in range(ROWS):
            inv = -1.0 / rem[0, q + 1, r + 1]
            ys = [rem[PLACE[s], q + 1, r + 1] for s in range(SPECIES)]
            rates.append(
                [
                    jnp.exp(thresh_s[s] * inv) * (ys[s] * ys[(s + 1) % SPECIES])
                    for s in range(SPECIES)
                ]
            )
        for i in range(FIELDS):
            f = ORDER[i]
            source = [None] * ROWS
            for s in range(SPECIES):
                m = mix[f * SPECIES + s]
                for r in range(ROWS):
                    term = m * rates[r][s]
                    source[r] = term if source[r] is None else source[r] + term
            mine = [rem[i, q + 1, r + 1] for r in range(ROWS)]
            for r in range(ROWS):
                x = mine[r]
                to_up = pltpu.roll(x, LANES - 1, 1)
                to_up = jnp.where(at_last, pltpu.roll(to_up, CHUNKS - 1, 0), to_up)
                to_low = pltpu.roll(x, 1, 1)
                to_low = jnp.where(at_first, pltpu.roll(to_low, 1, 0), to_low)
                total = 0.4 * x + gas[q, r] * source[r]
                total += coef[0, r] * rem[i, q + 2, r + 1] + coef[1, r] * rem[i, q, r + 1]
                total += coef[4, r] * to_up + coef[5, r] * to_low
                if r > 0:
                    total += coef[3, r] * mine[r - 1]
                if r < ROWS - 1:
                    total += coef[2, r] * mine[r + 1]
                out_ref(i)[q, row(r), :] = total

    def run_planes(first, count):
        def body(i, carry):
            plane(first + i)
            return carry

        lax.fori_loop(0, count, body, 0)

    run_planes(1, 4)
    each_down(range(2), False, lambda c: c.wait_recv())
    remap(0, 2, planes - 2, 3)
    xs_start(0, 1)
    xs_start(2, 0)
    pl.semaphore_wait(known.at[0], 2)
    greet(known.at[1], 2)
    run_planes(5, planes - 8)
    each_down(range(2, 4), False, lambda c: c.wait_recv())
    remap(2, 8, planes - 2, 2)
    xs_start(1, 1)
    xs_start(2, 1)
    pl.semaphore_wait(known.at[1], 2)
    greet(known.at[2], 4)
    each_up(range(4), False, lambda c: c.wait_recv())
    remap_low(0, FIELDS)
    run_planes(0, 1)
    run_planes(planes - 3, 1)
    each_down(range(4, 6), False, lambda c: c.wait_recv())
    remap(2, 8, planes, 1)
    run_planes(planes - 2, 2)

    def add_rows(group):
        f0, fn = GROUPS[group]

        def side(is_low):
            r = 0 if is_low else ROWS - 1
            halo = 0 if is_low else ROWS + 1

            def body(q, carry):
                c = edge[q, 0 if is_low else 1]
                for i in range(f0, f0 + fn):
                    ref = out_ref(i)
                    ref[q, row(r), :] = ref[q, row(r), :] + c * rem[i, q + 1, halo]
                return carry

            for span in range(2):
                xs_copy(group, span, not is_low).wait_recv()
            lax.fori_loop(0, planes, body, 0)

        @pl.when(xs > 0)
        def _():
            side(True)

        @pl.when(xs < n_xs - 1)
        def _():
            side(False)

    add_rows(0)

    def glow(q, sums):
        return tuple(
            sums[r]
            + gas[q, r] * out_ref(1)[q, row(r), :] * out_ref(0)[q, row(r), :]
            for r in range(ROWS)
        )

    zero = jnp.zeros((CHUNKS, LANES), jnp.float32)
    sums = lax.fori_loop(0, planes, glow, (zero,) * ROWS)
    for r in range(ROWS):
        img[pl.ds(r, CHUNKS, stride=CHUNKS), :] = sums[r]

    def img_copy(d):
        peer = lax.rem(ax + d, n_ax)
        tile = pl.ds(pl.multiple_of((peer // 2) * CHUNKS, CHUNKS), CHUNKS)
        return pltpu.make_async_remote_copy(
            src_ref=img.at[tile],
            dst_ref=img_in.at[d - 1],
            send_sem=img_send.at[d - 1],
            recv_sem=img_recv.at[d - 1],
            device_id=(peer, xs),
            device_id_type=MESH,
        )

    pl.semaphore_wait(known.at[2], 2)
    for d in range(1, n_ax):
        img_copy(d).start()

    add_rows(1)
    add_rows(2)

    mine = img[pl.ds(pl.multiple_of((ax // 2) * CHUNKS, CHUNKS), CHUNKS), :]
    for d in range(1, n_ax):
        img_copy(d).wait_recv()
        mine = mine + img_in[d - 1]
    half = LANES // 2
    mine = jnp.where(lax.rem(ax, 2) == 1, pltpu.roll(mine, half, 1), mine)
    image_out[...] = mine[:ROWS, :half] * (2.0 / total_planes) - picture_v[...]

    for d in range(1, n_ax):
        img_copy(d).wait_send()
    each_down(range(6), True, lambda c: c.wait_send())
    each_up(range(4), True, lambda c: c.wait_send())
    for group in range(3):
        for span in range(2):
            @pl.when(xs > 0)
            def _():
                xs_copy(group, span, True).wait_send()

            @pl.when(xs < n_xs - 1)
            def _():
                xs_copy(group, span, False).wait_send()


def tiled(x):
    *lead, rows, width = x.shape
    x = x.reshape(*lead, rows, width // LANES, LANES)
    return jnp.swapaxes(x, -3, -2).reshape(*lead, rows * (width // LANES), LANES)


def untiled(x, rows):
    *lead, both, lanes = x.shape
    x = x.reshape(*lead, both // rows, rows, lanes)
    return jnp.swapaxes(x, -3, -2).reshape(*lead, rows, (both // rows) * lanes)


def solution(mesh):
    n_ax, n_xs = mesh.shape["ax"], mesh.shape["xs"]

    def per_device(conc, temp, vel, gap, dest, rate_k, thresh, coeff, heat, picture):
        planes = conc.shape[1]
        total_planes = planes * n_ax
        f32 = jnp.float32
        any_space = pl.BlockSpec(memory_space=pltpu.HBM)
        vmem = pl.BlockSpec(memory_space=pltpu.VMEM)
        dma = pltpu.SemaphoreType.DMA
        both = ROWS * CHUNKS
        c, t, image = pl.pallas_call(
            functools.partial(per_device_kernel, n_ax, n_xs, planes, total_planes),
            out_shape=(
                jax.ShapeDtypeStruct((SPECIES, planes, both, LANES), f32),
                jax.ShapeDtypeStruct((planes, both, LANES), f32),
                jax.ShapeDtypeStruct(picture.shape, f32),
            ),
            in_specs=[any_space] * 10,
            out_specs=(vmem, vmem, vmem),
            scratch_shapes=[
                pltpu.VMEM((FIELDS, planes + 4, both, LANES), f32),
                pltpu.VMEM((FIELDS, planes + 2, ROWS + 2, CHUNKS, LANES), f32),
                pltpu.VMEM((3, planes, both, LANES), f32),
                pltpu.VMEM((planes, both, LANES), jnp.int32),
                pltpu.VMEM((6, ROWS, CHUNKS, LANES), f32),
                pltpu.VMEM((planes, 2, CHUNKS, LANES), f32),
                pltpu.VMEM((planes, ROWS, CHUNKS, LANES), f32),
                pltpu.SMEM((FIELDS * SPECIES,), f32),
                pltpu.VMEM((CHUNKS * CHUNKS, LANES), f32),
                pltpu.VMEM((n_ax - 1, CHUNKS, LANES), f32),
                dma((6,)),
                dma((6,)),
                dma((10,)),
                dma((10,)),
                dma((12,)),
                dma((12,)),
                dma((n_ax - 1,)),
                dma((n_ax - 1,)),
                pltpu.SemaphoreType.REGULAR((3,)),
                pltpu.SMEM(dest.shape, jnp.int32),
                pltpu.SMEM(rate_k.shape, f32),
                pltpu.SMEM(thresh.shape, f32),
                pltpu.SMEM(coeff.shape, f32),
                pltpu.SMEM(heat.shape, f32),
                pltpu.VMEM(picture.shape, f32),
            ],
            compiler_params=pltpu.CompilerParams(
                collective_id=0, has_side_effects=True, vmem_limit_bytes=24 * 1024 * 1024
            ),
            name="fused_step",
        )(
            *(
                pltpu.with_memory_space_constraint(x, pltpu.HBM)
                for x in (
                    tiled(conc), tiled(temp), tiled(vel), tiled(gap),
                    dest, rate_k, thresh, coeff, heat, picture,
                )
            )
        )
        return untiled(c, ROWS), untiled(t, ROWS), image

    in_specs = (
        P(None, "ax", "xs", None),
        P("ax", "xs", None),
        P(None, "ax", "xs", None),
        P("ax", "xs", None),
        P(),
        P(),
        P(),
        P(),
        P(),
        P("xs", "ax"),
    )
    out_specs = (P(None, "ax", "xs", None), P("ax", "xs", None), P("xs", "ax"))
    return jax.shard_map(
        per_device, mesh=mesh, in_specs=in_specs, out_specs=out_specs, check_vma=False
    )
```

```python
import functools

import jax
import jax.numpy as jnp
from jax import lax
from jax.experimental import pallas as pl
from jax.experimental.pallas import tpu as pltpu
from jax.sharding import PartitionSpec as P

SPECIES = 9
FIELDS = 10
ORDER = (9, 4, 0, 1, 2, 3, 5, 6, 7, 8)
PLACE = tuple(ORDER.index(f) for f in range(FIELDS))
GROUPS = ((0, 2), (2, 2), (4, 2), (6, 2), (8, 2))
RELAYED = (3, 4)
ROWS = 4
LANES = 128
CHUNKS = 8
MESH = pl.DeviceIdType.MESH


def per_device_kernel(
    n_ax, n_xs, planes, total_planes,
    conc, temp, vel, gap, dest, rate_k, thresh, coeff, heat, picture,
    conc_out, temp_out, image_out,
    old, rem, relay, pack, tail, vel_v, gap_v, coef, edge, gas, mix, img, img_in,
    load_sem, small_sem, ax_send, ax_recv, xs_send, xs_recv, relay_send, relay_recv, tail_send, tail_recv, img_send, img_recv,
    known, dest_s, rate_s, thresh_s, coeff_s, heat_s, picture_v,
):
    ax = lax.axis_index("ax")
    xs = lax.axis_index("xs")
    start = ax * planes

    barrier = pltpu.get_barrier_semaphore()
    def greet(semaphore, distance):
        @pl.when(ax >= distance)
        def _():
            pl.semaphore_signal(
                semaphore, inc=1, device_id=(ax - distance, xs), device_id_type=MESH
            )

        @pl.when(ax < n_ax - distance)
        def _():
            pl.semaphore_signal(
                semaphore, inc=1, device_id=(ax + distance, xs), device_id_type=MESH
            )

    def greeters(distance):
        return (ax >= distance).astype(jnp.int32) + (ax < n_ax - distance).astype(jnp.int32)

    greet(barrier, 1)
    has_low, has_high = xs > 0, xs < n_xs - 1
    middle = n_xs // 2
    below_middle, above_middle = xs == middle - 1, xs == middle

    def signal_xs(semaphore, target):
        pl.semaphore_signal(semaphore, inc=1, device_id=(ax, target), device_id_type=MESH)

    @pl.when(has_low)
    def _():
        signal_xs(barrier, xs - 1)

    @pl.when(has_high & ~below_middle)
    def _():
        signal_xs(barrier, xs + 1)

    far_slab, after_far = ax == n_ax // 2 - 1, ax == n_ax // 2

    @pl.when(above_middle & far_slab)
    def _():
        pl.semaphore_signal(
            barrier, inc=1, device_id=(ax + 1, middle - 1), device_id_type=MESH
        )

    @pl.when(xs == 0)
    def _():
        signal_xs(barrier, middle)
        signal_xs(barrier, middle - 1)

    @pl.when(xs == n_xs - 1)
    def _():
        signal_xs(barrier, middle - 1)

    def local(src, dst, sem):
        copy = pltpu.make_async_copy(src, dst, sem)
        copy.start()
        return copy

    smalls = [
        local(dest, dest_s, small_sem.at[0]),
        local(rate_k, rate_s, small_sem.at[1]),
        local(thresh, thresh_s, small_sem.at[2]),
        local(coeff, coeff_s, small_sem.at[3]),
        local(heat, heat_s, small_sem.at[4]),
        local(picture, picture_v, small_sem.at[5]),
    ]
    own = pl.ds(1, planes)
    loads = [
        local(temp, old.at[0, own], load_sem.at[0]),
        local(conc.at[4], old.at[1, own], load_sem.at[1]),
        local(conc.at[pl.ds(0, 4)], old.at[pl.ds(2, 4), own], load_sem.at[2]),
        local(conc.at[pl.ds(5, 4)], old.at[pl.ds(6, 4), own], load_sem.at[3]),
        local(vel, vel_v, load_sem.at[4]),
        local(gap, gap_v, load_sem.at[5]),
    ]

    @pl.when(ax == 0)
    def _():
        old[:, 0] = jnp.zeros((FIELDS, 32, LANES), jnp.float32)

    @pl.when(ax == n_ax - 1)
    def _():
        old[:, pl.ds(planes + 1, 3)] = jnp.zeros((FIELDS, 3, 32, LANES), jnp.float32)

    img[...] = jnp.zeros_like(img)

    def row(r):
        return pl.ds(r, CHUNKS, stride=ROWS)

    def weights(q):
        new = start + q

        def hit(k):
            p = jnp.clip(new + k, 0, total_planes - 1)
            good = (dest_s[p] == new) & (new + k < total_planes) & (new + k >= 0)
            return good.astype(jnp.int32)

        h = [hit(k) for k in range(3)]
        count = h[0] + h[1] + h[2]
        inv = jnp.where(count == 3, 1.0 / 3.0, jnp.where(count == 2, 0.5, 1.0)).astype(
            jnp.float32
        )
        inside = ((new >= 0) & (new < total_planes)).astype(jnp.int32)
        none = (count == 0).astype(jnp.int32) * inside
        first = (h[0] + none).astype(jnp.float32) * inv
        return first, h[1].astype(jnp.float32) * inv, h[2].astype(jnp.float32) * inv

    def remap(first_field, fields, q0, count):
        def body(i, carry):
            q = q0 + i
            w = weights(q)
            for f in range(first_field, first_field + fields):
                for r in range(ROWS):
                    rem[f, q + 1, r + 1] = (
                        w[0] * old[f, q + 1, row(r), :]
                        + w[1] * old[f, q + 2, row(r), :]
                        + w[2] * old[f, q + 3, row(r), :]
                    )
            return carry

        lax.fori_loop(0, count, body, 0)

    def remap_low(first_field, fields):
        w = weights(-1)
        for f in range(first_field, first_field + fields):
            for r in range(ROWS):
                rem[f, 0, r + 1] = (
                    w[0] * old[f, 0, row(r), :]
                    + w[1] * old[f, 1, row(r), :]
                    + w[2] * old[f, 2, row(r), :]
                )

    down = (lax.max(ax - 1, 0), xs)
    up = (lax.min(ax + 1, n_ax - 1), xs)
    low3, top3 = pl.ds(0, 3), pl.ds(planes + 1, 3)
    low2, top2 = pl.ds(0, 2), pl.ds(planes + 1, 2)
    firsts, lasts = pl.ds(0, 4), pl.ds(2, 4)
    seconds, ends = pl.ds(5, 4), pl.ds(6, 4)
    down_parts = (
        (temp.at[low3], (0, top3)),
        (conc.at[4, low3], (1, top3)),
        (conc.at[firsts, low2], (lasts, top2)),
        (conc.at[seconds, low2], (ends, top2)),
        (conc.at[firsts, 2], (lasts, planes + 3)),
        (conc.at[seconds, 2], (ends, planes + 3)),
    )
    up_parts = (
        (temp.at[planes - 1], (0, 0)),
        (conc.at[4, planes - 1], (1, 0)),
        (conc.at[firsts, planes - 1], (lasts, 0)),
        (conc.at[seconds, planes - 1], (ends, 0)),
    )

    def ax_copy(part, going_down):
        source, where = (down_parts if going_down else up_parts)[part]
        slot = part + (0 if going_down else len(down_parts))
        return pltpu.make_async_remote_copy(
            src_ref=source,
            dst_ref=old.at[where],
            send_sem=ax_send.at[slot],
            recv_sem=ax_recv.at[slot],
            device_id=down if going_down else up,
            device_id_type=MESH,
        )

    def each_down(parts, sending, act):
        @pl.when(ax > 0 if sending else ax < n_ax - 1)
        def _():
            for part in parts:
                act(ax_copy(part, True))

    def each_up(parts, sending, act):
        @pl.when(ax < n_ax - 1 if sending else ax > 0)
        def _():
            for part in parts:
                act(ax_copy(part, False))

    spans = (pl.ds(1, planes - 2), pl.ds(planes - 1, 2))

    def xs_copy(group, span, going_down):
        f0, fn = GROUPS[group]
        slot = 4 * group + 2 * span + (0 if going_down else 1)
        fields = pl.ds(f0, fn)
        return pltpu.make_async_remote_copy(
            src_ref=rem.at[fields, spans[span], 1 if going_down else ROWS],
            dst_ref=rem.at[fields, spans[span], ROWS + 1 if going_down else 0],
            send_sem=xs_send.at[slot],
            recv_sem=xs_recv.at[slot],
            device_id=(ax, lax.max(xs - 1, 0) if going_down else lax.min(xs + 1, n_xs - 1)),
            device_id_type=MESH,
        )

    def to_relay(group, going_down):
        f0, fn = GROUPS[group]
        slot = group - RELAYED[0]
        return pltpu.make_async_remote_copy(
            src_ref=rem.at[pl.ds(f0, fn), spans[0], 1 if going_down else ROWS],
            dst_ref=relay.at[pl.ds(2 * slot, fn)],
            send_sem=xs_send.at[4 * group + (0 if going_down else 1)],
            recv_sem=relay_recv.at[slot],
            device_id=(ax, 0 if going_down else n_xs - 1),
            device_id_type=MESH,
        )

    def from_relay(group, going_down):
        f0, fn = GROUPS[group]
        slot = group - RELAYED[0]
        return pltpu.make_async_remote_copy(
            src_ref=relay.at[pl.ds(2 * slot, fn)],
            dst_ref=rem.at[pl.ds(f0, fn), spans[0], ROWS + 1 if going_down else 0],
            send_sem=relay_send.at[slot],
            recv_sem=xs_recv.at[4 * group + (0 if going_down else 1)],
            device_id=(ax, middle - 1 if going_down else middle),
            device_id_type=MESH,
        )

    def goes_round(group):
        return (ax < n_ax - 2) | (group == RELAYED[-1])

    tail_fields = (pl.ds(0, 2), pl.ds(2, FIELDS - 2))

    def tail_copy(part, next_slab):
        fields = tail_fields[part]
        two = pl.ds(2 if next_slab else 0, 2)
        slot = 2 * part + (1 if next_slab else 0)
        return pltpu.make_async_remote_copy(
            src_ref=pack.at[fields, two],
            dst_ref=tail.at[fields, two],
            send_sem=tail_send.at[slot],
            recv_sem=tail_recv.at[slot],
            device_id=(lax.max(ax - 1, 0) if next_slab else ax, middle),
            device_id_type=MESH,
        )

    def tail_start(part):
        first, count = ((0, 2), (2, FIELDS - 2))[part]

        def send(next_slab, sources):
            for f in range(first, first + count):
                for k, p in sources:
                    pack[f, k] = old[f, p, row(ROWS - 1), :]
            tail_copy(part, next_slab).start()

        @pl.when(below_middle & far_slab)
        def _():
            send(False, ((0, planes - 1), (1, planes)))

        @pl.when(below_middle & after_far)
        def _():
            send(True, ((2, 1), (3, 2)))

    def tail_end():
        for next_slab, here in ((False, far_slab), (True, after_far)):
            @pl.when(below_middle & here)
            def _():
                for part in range(2):
                    tail_copy(part, next_slab).wait_send()

    def tail_rows(part):
        first, count = ((0, 2), (2, FIELDS - 2))[part]

        @pl.when(above_middle & far_slab)
        def _():
            tail_copy(part, True).wait_recv()
            tail_copy(part, False).wait_recv()
            for k in range(2):
                w = weights(planes - 2 + k)
                for f in range(first, first + count):
                    rem[f, planes - 1 + k, 0] = (
                        w[0] * tail[f, k] + w[1] * tail[f, k + 1] + w[2] * tail[f, k + 2]
                    )

    def middle_start(group):
        @pl.when(below_middle & goes_round(group))
        def _():
            to_relay(group, False).start()

        @pl.when(above_middle)
        def _():
            to_relay(group, True).start()

    def xs_start(group, span):
        @pl.when(has_low & ~above_middle)
        def _():
            xs_copy(group, span, True).start()

        relayed = group in RELAYED and span == 0

        elsewhere = goes_round(group) if relayed else far_slab

        @pl.when(has_high & ~(below_middle & elsewhere) if relayed or span == 1 else has_high)
        def _():
            xs_copy(group, span, False).start()

    def late_start():
        @pl.when(above_middle)
        def _():
            pl.semaphore_wait(known.at[4], 1)
            for group in range(5):
                for span in range(2):
                    if span == 1 or group not in RELAYED:
                        xs_copy(group, span, True).start()

    def pass_on(group, going_down):
        @pl.when((xs == (0 if going_down else n_xs - 1)) & (going_down | goes_round(group)))
        def _():
            if going_down and group == RELAYED[0]:
                pl.semaphore_wait(known.at[4], 1)
            to_relay(group, going_down).wait_recv()
            from_relay(group, going_down).start()

    def pass_end(going_down):
        for group in RELAYED:
            @pl.when((xs == (0 if going_down else n_xs - 1)) & (going_down | goes_round(group)))
            def _():
                from_relay(group, going_down).wait_send()

    greeted = greeters(1) + has_high.astype(jnp.int32) + (has_low & ~above_middle).astype(jnp.int32)
    pl.semaphore_wait(
        barrier,
        greeted
        + 2 * below_middle.astype(jnp.int32)
        + above_middle.astype(jnp.int32)
        + (below_middle & after_far).astype(jnp.int32),
    )
    each_down(range(6), True, lambda c: c.start())
    each_up(range(4), True, lambda c: c.start())

    @pl.when(below_middle)
    def _():
        signal_xs(known.at[4], middle)
        signal_xs(known.at[4], 0)

    smalls[0].wait()
    loads[0].wait()
    loads[1].wait()
    remap(0, 2, 0, planes - 2)
    xs_start(0, 0)
    tail_start(0)
    loads[2].wait()
    remap(2, 4, 0, planes - 2)
    xs_start(1, 0)
    loads[3].wait()
    remap(6, 4, 0, planes - 2)
    middle_start(3)
    middle_start(4)
    tail_start(1)
    greet(known.at[0], 1)
    for small in smalls[1:]:
        small.wait()
    loads[4].wait()
    loads[5].wait()

    for s in range(SPECIES):
        for r in range(SPECIES):
            mix[s * SPECIES + r] = coeff_s[s, r] * rate_s[r]
    for r in range(SPECIES):
        mix[SPECIES * SPECIES + r] = heat_s[r] * rate_s[r]

    lane = lax.broadcasted_iota(jnp.int32, (CHUNKS, LANES), 1)
    chunk = lax.broadcasted_iota(jnp.int32, (CHUNKS, LANES), 0)
    at_last = lane == LANES - 1
    at_first = lane == 0
    z_end = at_last & (chunk == CHUNKS - 1)
    z_begin = at_first & (chunk == 0)

    def out_ref(i):
        f = ORDER[i]
        return temp_out if f == SPECIES else conc_out.at[f]

    def plane(q, fields=range(FIELDS)):
        for r in range(ROWS):
            for d in range(3):
                v = 0.1 * vel_v[d, q, row(r), :]
                above = 0.1 - v
                below = 0.1 + v
                if d == 2:
                    above = jnp.where(z_end, 0.0, above)
                    below = jnp.where(z_begin, 0.0, below)
                if d == 1 and r == 0:
                    edge[q, 0] = below
                if d == 1 and r == ROWS - 1:
                    edge[q, 1] = above
                coef[2 * d, r] = above
                coef[2 * d + 1, r] = below
            gas[q, r] = 0.5 * (1 - gap_v[q, row(r), :]).astype(jnp.float32)
        rates = []
        for r in range(ROWS):
            inv = -1.0 / rem[0, q + 1, r + 1]
            ys = [rem[PLACE[s], q + 1, r + 1] for s in range(SPECIES)]
            rates.append(
                [
                    jnp.exp(thresh_s[s] * inv) * (ys[s] * ys[(s + 1) % SPECIES])
                    for s in range(SPECIES)
                ]
            )
        for i in fields:
            f = ORDER[i]
            source = [None] * ROWS
            for s in range(SPECIES):
                m = mix[f * SPECIES + s]
                for r in range(ROWS):
                    term = m * rates[r][s]
                    source[r] = term if source[r] is None else source[r] + term
            mine = [rem[i, q + 1, r + 1] for r in range(ROWS)]
            for r in range(ROWS):
                x = mine[r]
                to_up = pltpu.roll(x, LANES - 1, 1)
                to_up = jnp.where(at_last, pltpu.roll(to_up, CHUNKS - 1, 0), to_up)
                to_low = pltpu.roll(x, 1, 1)
                to_low = jnp.where(at_first, pltpu.roll(to_low, 1, 0), to_low)
                total = 0.4 * x + gas[q, r] * source[r]
                total += coef[0, r] * rem[i, q + 2, r + 1] + coef[1, r] * rem[i, q, r + 1]
                total += coef[4, r] * to_up + coef[5, r] * to_low
                if r > 0:
                    total += coef[3, r] * mine[r - 1]
                if r < ROWS - 1:
                    total += coef[2, r] * mine[r + 1]
                out_ref(i)[q, row(r), :] = total

    def run_planes(first, count):
        def body(i, carry):
            plane(first + i)
            return carry

        lax.fori_loop(0, count, body, 0)

    run_planes(1, 4)
    each_down(range(2), False, lambda c: c.wait_recv())
    remap(0, 2, planes - 2, 3)
    xs_start(0, 1)
    for group in range(2, 5):
        xs_start(group, 0)
    pl.semaphore_wait(known.at[0], greeters(1))
    greet(known.at[1], 2)
    pass_on(3, False)
    run_planes(5, planes - 8)
    pl.semaphore_wait(known.at[1], greeters(2))
    greet(known.at[2], 4)
    pass_on(4, False)
    each_down(range(2, 4), False, lambda c: c.wait_recv())
    remap(2, 8, planes - 2, 2)
    for group in range(1, 5):
        xs_start(group, 1)
    pl.semaphore_wait(known.at[2], greeters(4))
    greet(known.at[3], 8)
    each_up(range(4), False, lambda c: c.wait_recv())
    remap_low(0, FIELDS)
    run_planes(0, 1)
    run_planes(planes - 3, 2)
    plane(planes - 1, range(2))
    late_start()

    def add_rows(group):
        f0, fn = GROUPS[group]

        def side(is_low):
            r = 0 if is_low else ROWS - 1
            halo = 0 if is_low else ROWS + 1

            def body(q, carry):
                c = edge[q, 0 if is_low else 1]
                for i in range(f0, f0 + fn):
                    ref = out_ref(i)
                    ref[q, row(r), :] = ref[q, row(r), :] + c * rem[i, q + 1, halo]
                return carry

            xs_copy(group, 0, not is_low).wait_recv()
            if is_low:
                @pl.when(~(above_middle & far_slab))
                def _():
                    xs_copy(group, 1, False).wait_recv()
            else:
                xs_copy(group, 1, True).wait_recv()
            lax.fori_loop(0, planes, body, 0)

        @pl.when(xs > 0)
        def _():
            side(True)

        @pl.when(xs < n_xs - 1)
        def _():
            side(False)

    tail_rows(0)
    add_rows(0)

    def glow(q, sums):
        return tuple(
            sums[r]
            + gas[q, r] * out_ref(1)[q, row(r), :] * out_ref(0)[q, row(r), :]
            for r in range(ROWS)
        )

    zero = jnp.zeros((CHUNKS, LANES), jnp.float32)
    sums = lax.fori_loop(0, planes, glow, (zero,) * ROWS)
    for r in range(ROWS):
        img[pl.ds(r, CHUNKS, stride=CHUNKS), :] = sums[r]

    def img_copy(d):
        peer = lax.rem(ax + d, n_ax)
        tile = pl.ds(pl.multiple_of((peer // 2) * CHUNKS, CHUNKS), CHUNKS)
        return pltpu.make_async_remote_copy(
            src_ref=img.at[tile],
            dst_ref=img_in.at[d - 1],
            send_sem=img_send.at[d - 1],
            recv_sem=img_recv.at[d - 1],
            device_id=(peer, xs),
            device_id_type=MESH,
        )

    pl.semaphore_wait(known.at[3], greeters(8))
    for d in range(1, n_ax):
        img_copy(d).start()

    each_down(range(4, 6), False, lambda c: c.wait_recv())
    remap(2, 8, planes, 1)
    plane(planes - 1, range(2, FIELDS))
    tail_rows(1)
    for group in RELAYED:
        pass_on(group, True)
    for group in range(1, 5):
        add_rows(group)

    mine = img[pl.ds(pl.multiple_of((ax // 2) * CHUNKS, CHUNKS), CHUNKS), :]
    for d in range(1, n_ax):
        img_copy(d).wait_recv()
        mine = mine + img_in[d - 1]
    half = LANES // 2
    mine = jnp.where(lax.rem(ax, 2) == 1, pltpu.roll(mine, half, 1), mine)
    image_out[...] = mine[:ROWS, :half] * (2.0 / total_planes) - picture_v[...]

    for d in range(1, n_ax):
        img_copy(d).wait_send()
    each_down(range(6), True, lambda c: c.wait_send())
    each_up(range(4), True, lambda c: c.wait_send())
    tail_end()
    pass_end(False)
    pass_end(True)
    for group in range(5):
        for span in range(2):
            @pl.when(has_low)
            def _():
                xs_copy(group, span, True).wait_send()

            @pl.when(has_high & ~(below_middle & far_slab) if span == 1 else has_high)
            def _():
                xs_copy(group, span, False).wait_send()


def write_out(c, t, image, c_out, t_out, image_out, sem):
    copies = [
        pltpu.make_async_copy(c.at[pl.ds(3 * i, 3)], c_out.at[pl.ds(3 * i, 3)], sem.at[i])
        for i in range(3)
    ]
    copies.append(pltpu.make_async_copy(t, t_out, sem.at[3]))
    copies.append(pltpu.make_async_copy(image, image_out, sem.at[4]))
    for copy in copies:
        copy.start()
    for copy in copies:
        copy.wait()


def tiled(x):
    *lead, rows, width = x.shape
    x = x.reshape(*lead, rows, width // LANES, LANES)
    return jnp.swapaxes(x, -3, -2).reshape(*lead, rows * (width // LANES), LANES)


def untiled(x, rows):
    *lead, both, lanes = x.shape
    x = x.reshape(*lead, both // rows, rows, lanes)
    return jnp.swapaxes(x, -3, -2).reshape(*lead, rows, (both // rows) * lanes)


def solution(mesh):
    n_ax, n_xs = mesh.shape["ax"], mesh.shape["xs"]

    def per_device(conc, temp, vel, gap, dest, rate_k, thresh, coeff, heat, picture):
        planes = conc.shape[1]
        total_planes = planes * n_ax
        f32 = jnp.float32
        any_space = pl.BlockSpec(memory_space=pltpu.HBM)
        vmem = pl.BlockSpec(memory_space=pltpu.VMEM)
        dma = pltpu.SemaphoreType.DMA
        both = ROWS * CHUNKS
        c, t, image = pl.pallas_call(
            functools.partial(per_device_kernel, n_ax, n_xs, planes, total_planes),
            out_shape=(
                jax.ShapeDtypeStruct((SPECIES, planes, both, LANES), f32),
                jax.ShapeDtypeStruct((planes, both, LANES), f32),
                jax.ShapeDtypeStruct(picture.shape, f32),
            ),
            in_specs=[any_space] * 10,
            out_specs=(vmem, vmem, vmem),
            scratch_shapes=[
                pltpu.VMEM((FIELDS, planes + 4, both, LANES), f32),
                pltpu.VMEM((FIELDS, planes + 2, ROWS + 2, CHUNKS, LANES), f32),
                pltpu.VMEM((4, planes - 2, CHUNKS, LANES), f32),
                pltpu.VMEM((FIELDS, 4, CHUNKS, LANES), f32),
                pltpu.VMEM((FIELDS, 4, CHUNKS, LANES), f32),
                pltpu.VMEM((3, planes, both, LANES), f32),
                pltpu.VMEM((planes, both, LANES), jnp.int32),
                pltpu.VMEM((6, ROWS, CHUNKS, LANES), f32),
                pltpu.VMEM((planes, 2, CHUNKS, LANES), f32),
                pltpu.VMEM((planes, ROWS, CHUNKS, LANES), f32),
                pltpu.SMEM((FIELDS * SPECIES,), f32),
                pltpu.VMEM((CHUNKS * CHUNKS, LANES), f32),
                pltpu.VMEM((n_ax - 1, CHUNKS, LANES), f32),
                dma((6,)),
                dma((6,)),
                dma((10,)),
                dma((10,)),
                dma((20,)),
                dma((20,)),
                dma((2,)),
                dma((2,)),
                dma((4,)),
                dma((4,)),
                dma((n_ax - 1,)),
                dma((n_ax - 1,)),
                pltpu.SemaphoreType.REGULAR((5,)),
                pltpu.SMEM(dest.shape, jnp.int32),
                pltpu.SMEM(rate_k.shape, f32),
                pltpu.SMEM(thresh.shape, f32),
                pltpu.SMEM(coeff.shape, f32),
                pltpu.SMEM(heat.shape, f32),
                pltpu.VMEM(picture.shape, f32),
            ],
            compiler_params=pltpu.CompilerParams(
                collective_id=0, has_side_effects=True, vmem_limit_bytes=24 * 1024 * 1024
            ),
            name="fused_step",
        )(
            *(
                pltpu.with_memory_space_constraint(x, pltpu.HBM)
                for x in (
                    tiled(conc), tiled(temp), tiled(vel), tiled(gap),
                    dest, rate_k, thresh, coeff, heat, picture,
                )
            )
        )
        either = pl.BlockSpec(memory_space=pl.ANY)
        c, t, image = pl.pallas_call(
            write_out,
            out_shape=tuple(jax.ShapeDtypeStruct(x.shape, f32) for x in (c, t, image)),
            in_specs=[either] * 3,
            out_specs=(either,) * 3,
            scratch_shapes=[dma((5,))],
            compiler_params=pltpu.CompilerParams(vmem_limit_bytes=4 * 1024 * 1024),
            name="write_out",
        )(*(pltpu.with_memory_space_constraint(x, pltpu.VMEM) for x in (c, t, image)))
        return untiled(c, ROWS), untiled(t, ROWS), image

    in_specs = (
        P(None, "ax", "xs", None),
        P("ax", "xs", None),
        P(None, "ax", "xs", None),
        P("ax", "xs", None),
        P(),
        P(),
        P(),
        P(),
        P(),
        P("xs", "ax"),
    )
    out_specs = (P(None, "ax", "xs", None), P("ax", "xs", None), P("xs", "ax"))
    return jax.shard_map(
        per_device, mesh=mesh, in_specs=in_specs, out_specs=out_specs, check_vma=False
    )
```

```python
import functools

import jax
import jax.numpy as jnp
from jax import lax
from jax.experimental import pallas as pl
from jax.experimental.pallas import tpu as pltpu
from jax.sharding import PartitionSpec as P

SPECIES = 9
FIELDS = 10
ORDER = (9, 4, 0, 1, 2, 3, 5, 6, 7, 8)
PLACE = tuple(ORDER.index(f) for f in range(FIELDS))
GROUPS = ((0, 2), (2, 2), (4, 2), (6, 2), (8, 2))
RELAYED = (3, 4)
ROWS = 4
LANES = 128
CHUNKS = 8
MESH = pl.DeviceIdType.MESH


def per_device_kernel(
    n_ax, n_xs, planes, total_planes,
    conc, temp, vel, gap, dest, rate_k, thresh, coeff, heat, picture,
    conc_out, temp_out, image_out,
    old, rem, relay, pack, tail, vel_v, gap_v, coef, edge, gas, mix, img, img_in,
    load_sem, small_sem, ax_send, ax_recv, xs_send, xs_recv, relay_send, relay_recv, tail_send, tail_recv, img_send, img_recv,
    known, dest_s, rate_s, thresh_s, coeff_s, heat_s, picture_v,
):
    ax = lax.axis_index("ax")
    xs = lax.axis_index("xs")
    start = ax * planes

    barrier = pltpu.get_barrier_semaphore()
    def greet(semaphore, distance):
        @pl.when(ax >= distance)
        def _():
            pl.semaphore_signal(
                semaphore, inc=1, device_id=(ax - distance, xs), device_id_type=MESH
            )

        @pl.when(ax < n_ax - distance)
        def _():
            pl.semaphore_signal(
                semaphore, inc=1, device_id=(ax + distance, xs), device_id_type=MESH
            )

    def greeters(distance):
        return (ax >= distance).astype(jnp.int32) + (ax < n_ax - distance).astype(jnp.int32)

    greet(barrier, 1)
    has_low, has_high = xs > 0, xs < n_xs - 1
    middle = n_xs // 2
    below_middle, above_middle = xs == middle - 1, xs == middle

    def signal_xs(semaphore, target):
        pl.semaphore_signal(semaphore, inc=1, device_id=(ax, target), device_id_type=MESH)

    @pl.when(has_low)
    def _():
        signal_xs(barrier, xs - 1)

    @pl.when(has_high & ~below_middle)
    def _():
        signal_xs(barrier, xs + 1)

    far_slab, after_far = ax == n_ax // 2 - 1, ax == n_ax // 2

    @pl.when(above_middle & far_slab)
    def _():
        pl.semaphore_signal(
            barrier, inc=1, device_id=(ax + 1, middle - 1), device_id_type=MESH
        )

    @pl.when(xs == 0)
    def _():
        signal_xs(barrier, middle)
        signal_xs(barrier, middle - 1)

    @pl.when(xs == n_xs - 1)
    def _():
        signal_xs(barrier, middle - 1)

    def local(src, dst, sem):
        copy = pltpu.make_async_copy(src, dst, sem)
        copy.start()
        return copy

    smalls = [
        local(dest, dest_s, small_sem.at[0]),
        local(rate_k, rate_s, small_sem.at[1]),
        local(thresh, thresh_s, small_sem.at[2]),
        local(coeff, coeff_s, small_sem.at[3]),
        local(heat, heat_s, small_sem.at[4]),
        local(picture, picture_v, small_sem.at[5]),
    ]
    own = pl.ds(1, planes)
    loads = [
        local(temp, old.at[0, own], load_sem.at[0]),
        local(conc.at[4], old.at[1, own], load_sem.at[1]),
        local(conc.at[pl.ds(0, 4)], old.at[pl.ds(2, 4), own], load_sem.at[2]),
        local(conc.at[pl.ds(5, 4)], old.at[pl.ds(6, 4), own], load_sem.at[3]),
        local(vel, vel_v, load_sem.at[4]),
        local(gap, gap_v, load_sem.at[5]),
    ]

    @pl.when(ax == 0)
    def _():
        old[:, 0] = jnp.zeros((FIELDS, 32, LANES), jnp.float32)

    @pl.when(ax == n_ax - 1)
    def _():
        old[:, pl.ds(planes + 1, 3)] = jnp.zeros((FIELDS, 3, 32, LANES), jnp.float32)

    img[...] = jnp.zeros_like(img)

    def row(r):
        return pl.ds(r, CHUNKS, stride=ROWS)

    def weights(q):
        new = start + q

        def hit(k):
            p = jnp.clip(new + k, 0, total_planes - 1)
            good = (dest_s[p] == new) & (new + k < total_planes) & (new + k >= 0)
            return good.astype(jnp.int32)

        h = [hit(k) for k in range(3)]
        count = h[0] + h[1] + h[2]
        inv = jnp.where(count == 3, 1.0 / 3.0, jnp.where(count == 2, 0.5, 1.0)).astype(
            jnp.float32
        )
        inside = ((new >= 0) & (new < total_planes)).astype(jnp.int32)
        none = (count == 0).astype(jnp.int32) * inside
        first = (h[0] + none).astype(jnp.float32) * inv
        return first, h[1].astype(jnp.float32) * inv, h[2].astype(jnp.float32) * inv

    def remap(first_field, fields, q0, count):
        def body(i, carry):
            q = q0 + i
            w = weights(q)
            for f in range(first_field, first_field + fields):
                for r in range(ROWS):
                    rem[f, q + 1, r + 1] = (
                        w[0] * old[f, q + 1, row(r), :]
                        + w[1] * old[f, q + 2, row(r), :]
                        + w[2] * old[f, q + 3, row(r), :]
                    )
            return carry

        lax.fori_loop(0, count, body, 0)

    def remap_low(first_field, fields):
        w = weights(-1)
        for f in range(first_field, first_field + fields):
            for r in range(ROWS):
                rem[f, 0, r + 1] = (
                    w[0] * old[f, 0, row(r), :]
                    + w[1] * old[f, 1, row(r), :]
                    + w[2] * old[f, 2, row(r), :]
                )

    down = (lax.max(ax - 1, 0), xs)
    up = (lax.min(ax + 1, n_ax - 1), xs)
    low3, top3 = pl.ds(0, 3), pl.ds(planes + 1, 3)
    low2, top2 = pl.ds(0, 2), pl.ds(planes + 1, 2)
    firsts, lasts = pl.ds(0, 4), pl.ds(2, 4)
    seconds, ends = pl.ds(5, 4), pl.ds(6, 4)
    down_parts = (
        (temp.at[low3], (0, top3)),
        (conc.at[4, low3], (1, top3)),
        (conc.at[firsts, low2], (lasts, top2)),
        (conc.at[seconds, low2], (ends, top2)),
        (conc.at[firsts, 2], (lasts, planes + 3)),
        (conc.at[seconds, 2], (ends, planes + 3)),
    )
    up_parts = (
        (temp.at[planes - 1], (0, 0)),
        (conc.at[4, planes - 1], (1, 0)),
        (conc.at[firsts, planes - 1], (lasts, 0)),
        (conc.at[seconds, planes - 1], (ends, 0)),
    )

    def ax_copy(part, going_down):
        source, where = (down_parts if going_down else up_parts)[part]
        slot = part + (0 if going_down else len(down_parts))
        return pltpu.make_async_remote_copy(
            src_ref=source,
            dst_ref=old.at[where],
            send_sem=ax_send.at[slot],
            recv_sem=ax_recv.at[slot],
            device_id=down if going_down else up,
            device_id_type=MESH,
        )

    def each_down(parts, sending, act):
        @pl.when(ax > 0 if sending else ax < n_ax - 1)
        def _():
            for part in parts:
                act(ax_copy(part, True))

    def each_up(parts, sending, act):
        @pl.when(ax < n_ax - 1 if sending else ax > 0)
        def _():
            for part in parts:
                act(ax_copy(part, False))

    spans = (pl.ds(1, planes - 2), pl.ds(planes - 1, 2))

    def xs_copy(group, span, going_down):
        f0, fn = GROUPS[group]
        slot = 4 * group + 2 * span + (0 if going_down else 1)
        fields = pl.ds(f0, fn)
        return pltpu.make_async_remote_copy(
            src_ref=rem.at[fields, spans[span], 1 if going_down else ROWS],
            dst_ref=rem.at[fields, spans[span], ROWS + 1 if going_down else 0],
            send_sem=xs_send.at[slot],
            recv_sem=xs_recv.at[slot],
            device_id=(ax, lax.max(xs - 1, 0) if going_down else lax.min(xs + 1, n_xs - 1)),
            device_id_type=MESH,
        )

    def to_relay(group, going_down):
        f0, fn = GROUPS[group]
        slot = group - RELAYED[0]
        return pltpu.make_async_remote_copy(
            src_ref=rem.at[pl.ds(f0, fn), spans[0], 1 if going_down else ROWS],
            dst_ref=relay.at[pl.ds(2 * slot, fn)],
            send_sem=xs_send.at[4 * group + (0 if going_down else 1)],
            recv_sem=relay_recv.at[slot],
            device_id=(ax, 0 if going_down else n_xs - 1),
            device_id_type=MESH,
        )

    def from_relay(group, going_down):
        f0, fn = GROUPS[group]
        slot = group - RELAYED[0]
        return pltpu.make_async_remote_copy(
            src_ref=relay.at[pl.ds(2 * slot, fn)],
            dst_ref=rem.at[pl.ds(f0, fn), spans[0], ROWS + 1 if going_down else 0],
            send_sem=relay_send.at[slot],
            recv_sem=xs_recv.at[4 * group + (0 if going_down else 1)],
            device_id=(ax, middle - 1 if going_down else middle),
            device_id_type=MESH,
        )

    def goes_round(group):
        return (ax < n_ax - 2) | (group == RELAYED[-1])

    tail_fields = (pl.ds(0, 2), pl.ds(2, FIELDS - 2))

    def tail_copy(part, next_slab):
        fields = tail_fields[part]
        two = pl.ds(2 if next_slab else 0, 2)
        slot = 2 * part + (1 if next_slab else 0)
        return pltpu.make_async_remote_copy(
            src_ref=pack.at[fields, two],
            dst_ref=tail.at[fields, two],
            send_sem=tail_send.at[slot],
            recv_sem=tail_recv.at[slot],
            device_id=(lax.max(ax - 1, 0) if next_slab else ax, middle),
            device_id_type=MESH,
        )

    def tail_start(part):
        first, count = ((0, 2), (2, FIELDS - 2))[part]

        def send(next_slab, sources):
            for f in range(first, first + count):
                for k, p in sources:
                    pack[f, k] = old[f, p, row(ROWS - 1), :]
            tail_copy(part, next_slab).start()

        @pl.when(below_middle & far_slab)
        def _():
            send(False, ((0, planes - 1), (1, planes)))

        @pl.when(below_middle & after_far)
        def _():
            send(True, ((2, 1), (3, 2)))

    def tail_end():
        for next_slab, here in ((False, far_slab), (True, after_far)):
            @pl.when(below_middle & here)
            def _():
                for part in range(2):
                    tail_copy(part, next_slab).wait_send()

    def tail_rows(part):
        first, count = ((0, 2), (2, FIELDS - 2))[part]

        @pl.when(above_middle & far_slab)
        def _():
            tail_copy(part, True).wait_recv()
            tail_copy(part, False).wait_recv()
            for k in range(2):
                w = weights(planes - 2 + k)
                for f in range(first, first + count):
                    rem[f, planes - 1 + k, 0] = (
                        w[0] * tail[f, k] + w[1] * tail[f, k + 1] + w[2] * tail[f, k + 2]
                    )

    def middle_start(group):
        @pl.when(below_middle & goes_round(group))
        def _():
            to_relay(group, False).start()

        @pl.when(above_middle)
        def _():
            to_relay(group, True).start()

    def xs_start(group, span):
        @pl.when(has_low & ~above_middle)
        def _():
            xs_copy(group, span, True).start()

        relayed = group in RELAYED and span == 0

        elsewhere = goes_round(group) if relayed else far_slab

        @pl.when(has_high & ~(below_middle & elsewhere) if relayed or span == 1 else has_high)
        def _():
            xs_copy(group, span, False).start()

    def late_start():
        @pl.when(above_middle)
        def _():
            pl.semaphore_wait(known.at[4], 1)
            for group in range(5):
                for span in range(2):
                    if span == 1 or group not in RELAYED:
                        xs_copy(group, span, True).start()

    def pass_on(group, going_down):
        @pl.when((xs == (0 if going_down else n_xs - 1)) & (going_down | goes_round(group)))
        def _():
            if going_down and group == RELAYED[0]:
                pl.semaphore_wait(known.at[4], 1)
            to_relay(group, going_down).wait_recv()
            from_relay(group, going_down).start()

    def pass_end(going_down):
        for group in RELAYED:
            @pl.when((xs == (0 if going_down else n_xs - 1)) & (going_down | goes_round(group)))
            def _():
                from_relay(group, going_down).wait_send()

    smalls[0].wait()
    loads[0].wait()
    loads[1].wait()
    remap(0, 2, 0, planes - 2)
    greeted = greeters(1) + has_high.astype(jnp.int32) + (has_low & ~above_middle).astype(jnp.int32)
    pl.semaphore_wait(
        barrier,
        greeted
        + 2 * below_middle.astype(jnp.int32)
        + above_middle.astype(jnp.int32)
        + (below_middle & after_far).astype(jnp.int32),
    )
    xs_start(0, 0)
    each_down(range(2), True, lambda c: c.start())
    tail_start(0)
    each_down(range(2, 6), True, lambda c: c.start())

    @pl.when(below_middle)
    def _():
        signal_xs(known.at[4], middle)
        signal_xs(known.at[4], 0)

    loads[2].wait()
    remap(2, 4, 0, planes - 2)
    xs_start(1, 0)
    loads[3].wait()
    remap(6, 4, 0, planes - 2)
    middle_start(3)
    middle_start(4)
    tail_start(1)
    each_up(range(4), True, lambda c: c.start())
    greet(known.at[0], 1)
    for small in smalls[1:]:
        small.wait()
    loads[4].wait()
    loads[5].wait()

    for s in range(SPECIES):
        for r in range(SPECIES):
            mix[s * SPECIES + r] = coeff_s[s, r] * rate_s[r]
    for r in range(SPECIES):
        mix[SPECIES * SPECIES + r] = heat_s[r] * rate_s[r]

    lane = lax.broadcasted_iota(jnp.int32, (CHUNKS, LANES), 1)
    chunk = lax.broadcasted_iota(jnp.int32, (CHUNKS, LANES), 0)
    at_last = lane == LANES - 1
    at_first = lane == 0
    z_end = at_last & (chunk == CHUNKS - 1)
    z_begin = at_first & (chunk == 0)

    def out_ref(i):
        f = ORDER[i]
        return temp_out if f == SPECIES else conc_out.at[f]

    def plane(q, fields=range(FIELDS)):
        for r in range(ROWS):
            for d in range(3):
                v = 0.1 * vel_v[d, q, row(r), :]
                above = 0.1 - v
                below = 0.1 + v
                if d == 2:
                    above = jnp.where(z_end, 0.0, above)
                    below = jnp.where(z_begin, 0.0, below)
                if d == 1 and r == 0:
                    edge[q, 0] = below
                if d == 1 and r == ROWS - 1:
                    edge[q, 1] = above
                coef[2 * d, r] = above
                coef[2 * d + 1, r] = below
            gas[q, r] = 0.5 * (1 - gap_v[q, row(r), :]).astype(jnp.float32)
        rates = []
        for r in range(ROWS):
            inv = -1.0 / rem[0, q + 1, r + 1]
            ys = [rem[PLACE[s], q + 1, r + 1] for s in range(SPECIES)]
            rates.append(
                [
                    jnp.exp(thresh_s[s] * inv) * (ys[s] * ys[(s + 1) % SPECIES])
                    for s in range(SPECIES)
                ]
            )
        for i in fields:
            f = ORDER[i]
            source = [None] * ROWS
            for s in range(SPECIES):
                m = mix[f * SPECIES + s]
                for r in range(ROWS):
                    term = m * rates[r][s]
                    source[r] = term if source[r] is None else source[r] + term
            mine = [rem[i, q + 1, r + 1] for r in range(ROWS)]
            for r in range(ROWS):
                x = mine[r]
                to_up = pltpu.roll(x, LANES - 1, 1)
                to_up = jnp.where(at_last, pltpu.roll(to_up, CHUNKS - 1, 0), to_up)
                to_low = pltpu.roll(x, 1, 1)
                to_low = jnp.where(at_first, pltpu.roll(to_low, 1, 0), to_low)
                total = 0.4 * x + gas[q, r] * source[r]
                total += coef[0, r] * rem[i, q + 2, r + 1] + coef[1, r] * rem[i, q, r + 1]
                total += coef[4, r] * to_up + coef[5, r] * to_low
                if r > 0:
                    total += coef[3, r] * mine[r - 1]
                if r < ROWS - 1:
                    total += coef[2, r] * mine[r + 1]
                out_ref(i)[q, row(r), :] = total

    def run_planes(first, count):
        def body(i, carry):
            plane(first + i)
            return carry

        lax.fori_loop(0, count, body, 0)

    run_planes(1, 4)
    each_down(range(2), False, lambda c: c.wait_recv())
    remap(0, 2, planes - 2, 3)
    xs_start(0, 1)
    for group in range(2, 5):
        xs_start(group, 0)
    pl.semaphore_wait(known.at[0], greeters(1))
    greet(known.at[1], 2)
    pass_on(3, False)
    run_planes(5, planes - 8)
    pl.semaphore_wait(known.at[1], greeters(2))
    greet(known.at[2], 4)
    pass_on(4, False)
    each_down(range(2, 4), False, lambda c: c.wait_recv())
    remap(2, 8, planes - 2, 2)
    for group in range(1, 5):
        xs_start(group, 1)
    pl.semaphore_wait(known.at[2], greeters(4))
    greet(known.at[3], 8)
    each_up(range(4), False, lambda c: c.wait_recv())
    remap_low(0, FIELDS)
    run_planes(0, 1)
    run_planes(planes - 3, 2)
    plane(planes - 1, range(2))
    late_start()

    def add_rows(group):
        f0, fn = GROUPS[group]

        def side(is_low):
            r = 0 if is_low else ROWS - 1
            halo = 0 if is_low else ROWS + 1

            def body(q, carry):
                c = edge[q, 0 if is_low else 1]
                for i in range(f0, f0 + fn):
                    ref = out_ref(i)
                    ref[q, row(r), :] = ref[q, row(r), :] + c * rem[i, q + 1, halo]
                return carry

            xs_copy(group, 0, not is_low).wait_recv()
            if is_low:
                @pl.when(~(above_middle & far_slab))
                def _():
                    xs_copy(group, 1, False).wait_recv()
            else:
                xs_copy(group, 1, True).wait_recv()
            lax.fori_loop(0, planes, body, 0)

        @pl.when(xs > 0)
        def _():
            side(True)

        @pl.when(xs < n_xs - 1)
        def _():
            side(False)

    tail_rows(0)
    add_rows(0)

    def glow(q, sums):
        return tuple(
            sums[r]
            + gas[q, r] * out_ref(1)[q, row(r), :] * out_ref(0)[q, row(r), :]
            for r in range(ROWS)
        )

    zero = jnp.zeros((CHUNKS, LANES), jnp.float32)
    sums = lax.fori_loop(0, planes, glow, (zero,) * ROWS)
    for r in range(ROWS):
        img[pl.ds(r, CHUNKS, stride=CHUNKS), :] = sums[r]

    def img_copy(d):
        peer = lax.rem(ax + d, n_ax)
        tile = pl.ds(pl.multiple_of((peer // 2) * CHUNKS, CHUNKS), CHUNKS)
        return pltpu.make_async_remote_copy(
            src_ref=img.at[tile],
            dst_ref=img_in.at[d - 1],
            send_sem=img_send.at[d - 1],
            recv_sem=img_recv.at[d - 1],
            device_id=(peer, xs),
            device_id_type=MESH,
        )

    pl.semaphore_wait(known.at[3], greeters(8))
    for d in sorted(range(1, n_ax), key=lambda d: abs(d - n_ax // 2)):
        img_copy(d).start()

    each_down(range(4, 6), False, lambda c: c.wait_recv())
    remap(2, 8, planes, 1)
    plane(planes - 1, range(2, FIELDS))
    tail_rows(1)
    for group in RELAYED:
        pass_on(group, True)
    for group in range(1, 5):
        add_rows(group)

    mine = img[pl.ds(pl.multiple_of((ax // 2) * CHUNKS, CHUNKS), CHUNKS), :]
    for d in range(1, n_ax):
        img_copy(d).wait_recv()
        mine = mine + img_in[d - 1]
    half = LANES // 2
    mine = jnp.where(lax.rem(ax, 2) == 1, pltpu.roll(mine, half, 1), mine)
    image_out[...] = mine[:ROWS, :half] * (2.0 / total_planes) - picture_v[...]

    for d in range(1, n_ax):
        img_copy(d).wait_send()
    each_down(range(6), True, lambda c: c.wait_send())
    each_up(range(4), True, lambda c: c.wait_send())
    tail_end()
    pass_end(False)
    pass_end(True)
    for group in range(5):
        for span in range(2):
            @pl.when(has_low)
            def _():
                xs_copy(group, span, True).wait_send()

            @pl.when(has_high & ~(below_middle & far_slab) if span == 1 else has_high)
            def _():
                xs_copy(group, span, False).wait_send()


def write_out(c, t, image, c_out, t_out, image_out, sem):
    copies = [
        pltpu.make_async_copy(c.at[pl.ds(3 * i, 3)], c_out.at[pl.ds(3 * i, 3)], sem.at[i])
        for i in range(3)
    ]
    copies.append(pltpu.make_async_copy(t, t_out, sem.at[3]))
    copies.append(pltpu.make_async_copy(image, image_out, sem.at[4]))
    for copy in copies:
        copy.start()
    for copy in copies:
        copy.wait()


def tiled(x):
    *lead, rows, width = x.shape
    x = x.reshape(*lead, rows, width // LANES, LANES)
    return jnp.swapaxes(x, -3, -2).reshape(*lead, rows * (width // LANES), LANES)


def untiled(x, rows):
    *lead, both, lanes = x.shape
    x = x.reshape(*lead, both // rows, rows, lanes)
    return jnp.swapaxes(x, -3, -2).reshape(*lead, rows, (both // rows) * lanes)


def solution(mesh):
    n_ax, n_xs = mesh.shape["ax"], mesh.shape["xs"]

    def per_device(conc, temp, vel, gap, dest, rate_k, thresh, coeff, heat, picture):
        planes = conc.shape[1]
        total_planes = planes * n_ax
        f32 = jnp.float32
        any_space = pl.BlockSpec(memory_space=pltpu.HBM)
        vmem = pl.BlockSpec(memory_space=pltpu.VMEM)
        dma = pltpu.SemaphoreType.DMA
        both = ROWS * CHUNKS
        c, t, image = pl.pallas_call(
            functools.partial(per_device_kernel, n_ax, n_xs, planes, total_planes),
            out_shape=(
                jax.ShapeDtypeStruct((SPECIES, planes, both, LANES), f32),
                jax.ShapeDtypeStruct((planes, both, LANES), f32),
                jax.ShapeDtypeStruct(picture.shape, f32),
            ),
            in_specs=[any_space] * 10,
            out_specs=(vmem, vmem, vmem),
            scratch_shapes=[
                pltpu.VMEM((FIELDS, planes + 4, both, LANES), f32),
                pltpu.VMEM((FIELDS, planes + 2, ROWS + 2, CHUNKS, LANES), f32),
                pltpu.VMEM((4, planes - 2, CHUNKS, LANES), f32),
                pltpu.VMEM((FIELDS, 4, CHUNKS, LANES), f32),
                pltpu.VMEM((FIELDS, 4, CHUNKS, LANES), f32),
                pltpu.VMEM((3, planes, both, LANES), f32),
                pltpu.VMEM((planes, both, LANES), jnp.int32),
                pltpu.VMEM((6, ROWS, CHUNKS, LANES), f32),
                pltpu.VMEM((planes, 2, CHUNKS, LANES), f32),
                pltpu.VMEM((planes, ROWS, CHUNKS, LANES), f32),
                pltpu.SMEM((FIELDS * SPECIES,), f32),
                pltpu.VMEM((CHUNKS * CHUNKS, LANES), f32),
                pltpu.VMEM((n_ax - 1, CHUNKS, LANES), f32),
                dma((6,)),
                dma((6,)),
                dma((10,)),
                dma((10,)),
                dma((20,)),
                dma((20,)),
                dma((2,)),
                dma((2,)),
                dma((4,)),
                dma((4,)),
                dma((n_ax - 1,)),
                dma((n_ax - 1,)),
                pltpu.SemaphoreType.REGULAR((5,)),
                pltpu.SMEM(dest.shape, jnp.int32),
                pltpu.SMEM(rate_k.shape, f32),
                pltpu.SMEM(thresh.shape, f32),
                pltpu.SMEM(coeff.shape, f32),
                pltpu.SMEM(heat.shape, f32),
                pltpu.VMEM(picture.shape, f32),
            ],
            compiler_params=pltpu.CompilerParams(
                collective_id=0, has_side_effects=True, vmem_limit_bytes=24 * 1024 * 1024
            ),
            name="fused_step",
        )(
            *(
                pltpu.with_memory_space_constraint(x, pltpu.HBM)
                for x in (
                    tiled(conc), tiled(temp), tiled(vel), tiled(gap),
                    dest, rate_k, thresh, coeff, heat, picture,
                )
            )
        )
        either = pl.BlockSpec(memory_space=pl.ANY)
        c, t, image = pl.pallas_call(
            write_out,
            out_shape=tuple(jax.ShapeDtypeStruct(x.shape, f32) for x in (c, t, image)),
            in_specs=[either] * 3,
            out_specs=(either,) * 3,
            scratch_shapes=[dma((5,))],
            compiler_params=pltpu.CompilerParams(vmem_limit_bytes=4 * 1024 * 1024),
            name="write_out",
        )(*(pltpu.with_memory_space_constraint(x, pltpu.VMEM) for x in (c, t, image)))
        return untiled(c, ROWS), untiled(t, ROWS), image

    in_specs = (
        P(None, "ax", "xs", None),
        P("ax", "xs", None),
        P(None, "ax", "xs", None),
        P("ax", "xs", None),
        P(),
        P(),
        P(),
        P(),
        P(),
        P("xs", "ax"),
    )
    out_specs = (P(None, "ax", "xs", None), P("ax", "xs", None), P("xs", "ax"))
    return jax.shard_map(
        per_device, mesh=mesh, in_specs=in_specs, out_specs=out_specs, check_vma=False
    )
```

```python
import functools

import jax
import jax.numpy as jnp
from jax import lax
from jax.experimental import pallas as pl
from jax.experimental.pallas import tpu as pltpu
from jax.sharding import PartitionSpec as P

SPECIES = 9
FIELDS = 10
ORDER = (9, 4, 0, 1, 2, 3, 5, 6, 7, 8)
PLACE = tuple(ORDER.index(f) for f in range(FIELDS))
GROUPS = ((0, 2), (2, 2), (4, 2), (6, 2), (8, 2))
RELAYED = (3, 4)
ROWS = 4
LANES = 128
CHUNKS = 8
MESH = pl.DeviceIdType.MESH


def per_device_kernel(
    n_ax, n_xs, planes, total_planes,
    conc, temp, vel, gap, dest, rate_k, thresh, coeff, heat, picture,
    conc_out, temp_out, image_out,
    old, rem, relay, pack, tail, vel_v, gap_v, coef, edge, gas, mix, img, img_in,
    load_sem, small_sem, ax_send, ax_recv, xs_send, xs_recv, relay_send, relay_recv, tail_send, tail_recv, img_send, img_recv,
    known, dest_s, rate_s, thresh_s, coeff_s, heat_s, picture_v,
):
    ax = lax.axis_index("ax")
    xs = lax.axis_index("xs")
    start = ax * planes

    barrier = pltpu.get_barrier_semaphore()
    def greet(semaphore, distance):
        @pl.when(ax >= distance)
        def _():
            pl.semaphore_signal(
                semaphore, inc=1, device_id=(ax - distance, xs), device_id_type=MESH
            )

        @pl.when(ax < n_ax - distance)
        def _():
            pl.semaphore_signal(
                semaphore, inc=1, device_id=(ax + distance, xs), device_id_type=MESH
            )

    def greeters(distance):
        return (ax >= distance).astype(jnp.int32) + (ax < n_ax - distance).astype(jnp.int32)

    greet(barrier, 1)
    has_low, has_high = xs > 0, xs < n_xs - 1
    middle = n_xs // 2
    below_middle, above_middle = xs == middle - 1, xs == middle

    def signal_xs(semaphore, target):
        pl.semaphore_signal(semaphore, inc=1, device_id=(ax, target), device_id_type=MESH)

    @pl.when(has_low)
    def _():
        signal_xs(barrier, xs - 1)

    @pl.when(has_high & ~below_middle)
    def _():
        signal_xs(barrier, xs + 1)

    far_slab, after_far = ax == n_ax // 2 - 1, ax == n_ax // 2

    @pl.when(above_middle & far_slab)
    def _():
        pl.semaphore_signal(
            barrier, inc=1, device_id=(ax + 1, middle - 1), device_id_type=MESH
        )

    @pl.when(xs == 0)
    def _():
        signal_xs(barrier, middle)
        signal_xs(barrier, middle - 1)

    @pl.when(xs == n_xs - 1)
    def _():
        signal_xs(barrier, middle - 1)

    def local(src, dst, sem):
        copy = pltpu.make_async_copy(src, dst, sem)
        copy.start()
        return copy

    smalls = [
        local(dest, dest_s, small_sem.at[0]),
        local(rate_k, rate_s, small_sem.at[1]),
        local(thresh, thresh_s, small_sem.at[2]),
        local(coeff, coeff_s, small_sem.at[3]),
        local(heat, heat_s, small_sem.at[4]),
        local(picture, picture_v, small_sem.at[5]),
    ]
    own = pl.ds(1, planes)
    loads = [
        local(temp, old.at[0, own], load_sem.at[0]),
        local(conc.at[4], old.at[1, own], load_sem.at[1]),
        local(conc.at[pl.ds(0, 4)], old.at[pl.ds(2, 4), own], load_sem.at[2]),
        local(conc.at[pl.ds(5, 4)], old.at[pl.ds(6, 4), own], load_sem.at[3]),
        local(vel, vel_v, load_sem.at[4]),
        local(gap, gap_v, load_sem.at[5]),
    ]

    @pl.when(ax == 0)
    def _():
        old[:, 0] = jnp.zeros((FIELDS, 32, LANES), jnp.float32)

    @pl.when(ax == n_ax - 1)
    def _():
        old[:, pl.ds(planes + 1, 3)] = jnp.zeros((FIELDS, 3, 32, LANES), jnp.float32)

    img[...] = jnp.zeros_like(img)

    def row(r):
        return pl.ds(r, CHUNKS, stride=ROWS)

    def weights(q):
        new = start + q

        def hit(k):
            p = jnp.clip(new + k, 0, total_planes - 1)
            good = (dest_s[p] == new) & (new + k < total_planes) & (new + k >= 0)
            return good.astype(jnp.int32)

        h = [hit(k) for k in range(3)]
        count = h[0] + h[1] + h[2]
        inv = jnp.where(count == 3, 1.0 / 3.0, jnp.where(count == 2, 0.5, 1.0)).astype(
            jnp.float32
        )
        inside = ((new >= 0) & (new < total_planes)).astype(jnp.int32)
        none = (count == 0).astype(jnp.int32) * inside
        first = (h[0] + none).astype(jnp.float32) * inv
        return first, h[1].astype(jnp.float32) * inv, h[2].astype(jnp.float32) * inv

    def remap(first_field, fields, q0, count):
        def body(i, carry):
            q = q0 + i
            w = weights(q)
            for f in range(first_field, first_field + fields):
                for r in range(ROWS):
                    rem[f, q + 1, r + 1] = (
                        w[0] * old[f, q + 1, row(r), :]
                        + w[1] * old[f, q + 2, row(r), :]
                        + w[2] * old[f, q + 3, row(r), :]
                    )
            return carry

        lax.fori_loop(0, count, body, 0)

    def remap_low(first_field, fields):
        w = weights(-1)
        for f in range(first_field, first_field + fields):
            for r in range(ROWS):
                rem[f, 0, r + 1] = (
                    w[0] * old[f, 0, row(r), :]
                    + w[1] * old[f, 1, row(r), :]
                    + w[2] * old[f, 2, row(r), :]
                )

    down = (lax.max(ax - 1, 0), xs)
    up = (lax.min(ax + 1, n_ax - 1), xs)
    low3, top3 = pl.ds(0, 3), pl.ds(planes + 1, 3)
    low2, top2 = pl.ds(0, 2), pl.ds(planes + 1, 2)
    firsts, lasts = pl.ds(0, 4), pl.ds(2, 4)
    seconds, ends = pl.ds(5, 4), pl.ds(6, 4)
    down_parts = (
        (temp.at[low3], (0, top3)),
        (conc.at[4, low3], (1, top3)),
        (conc.at[firsts, low2], (lasts, top2)),
        (conc.at[seconds, low2], (ends, top2)),
        (conc.at[firsts, 2], (lasts, planes + 3)),
        (conc.at[seconds, 2], (ends, planes + 3)),
    )
    up_parts = (
        (temp.at[planes - 1], (0, 0)),
        (conc.at[4, planes - 1], (1, 0)),
        (conc.at[firsts, planes - 1], (lasts, 0)),
        (conc.at[seconds, planes - 1], (ends, 0)),
    )

    def ax_copy(part, going_down):
        source, where = (down_parts if going_down else up_parts)[part]
        slot = part + (0 if going_down else len(down_parts))
        return pltpu.make_async_remote_copy(
            src_ref=source,
            dst_ref=old.at[where],
            send_sem=ax_send.at[slot],
            recv_sem=ax_recv.at[slot],
            device_id=down if going_down else up,
            device_id_type=MESH,
        )

    def each_down(parts, sending, act):
        @pl.when(ax > 0 if sending else ax < n_ax - 1)
        def _():
            for part in parts:
                act(ax_copy(part, True))

    def each_up(parts, sending, act):
        @pl.when(ax < n_ax - 1 if sending else ax > 0)
        def _():
            for part in parts:
                act(ax_copy(part, False))

    spans = (pl.ds(1, planes - 2), pl.ds(planes - 1, 2))

    def xs_copy(group, span, going_down):
        f0, fn = GROUPS[group]
        slot = 4 * group + 2 * span + (0 if going_down else 1)
        fields = pl.ds(f0, fn)
        return pltpu.make_async_remote_copy(
            src_ref=rem.at[fields, spans[span], 1 if going_down else ROWS],
            dst_ref=rem.at[fields, spans[span], ROWS + 1 if going_down else 0],
            send_sem=xs_send.at[slot],
            recv_sem=xs_recv.at[slot],
            device_id=(ax, lax.max(xs - 1, 0) if going_down else lax.min(xs + 1, n_xs - 1)),
            device_id_type=MESH,
        )

    def to_relay(group, going_down):
        f0, fn = GROUPS[group]
        slot = group - RELAYED[0]
        return pltpu.make_async_remote_copy(
            src_ref=rem.at[pl.ds(f0, fn), spans[0], 1 if going_down else ROWS],
            dst_ref=relay.at[pl.ds(2 * slot, fn)],
            send_sem=xs_send.at[4 * group + (0 if going_down else 1)],
            recv_sem=relay_recv.at[slot],
            device_id=(ax, 0 if going_down else n_xs - 1),
            device_id_type=MESH,
        )

    def from_relay(group, going_down):
        f0, fn = GROUPS[group]
        slot = group - RELAYED[0]
        return pltpu.make_async_remote_copy(
            src_ref=relay.at[pl.ds(2 * slot, fn)],
            dst_ref=rem.at[pl.ds(f0, fn), spans[0], ROWS + 1 if going_down else 0],
            send_sem=relay_send.at[slot],
            recv_sem=xs_recv.at[4 * group + (0 if going_down else 1)],
            device_id=(ax, middle - 1 if going_down else middle),
            device_id_type=MESH,
        )

    def goes_round(group):
        return (ax < n_ax - 2) | (group == RELAYED[-1])

    tail_fields = (pl.ds(0, 2), pl.ds(2, FIELDS - 2))

    def tail_copy(part, next_slab):
        fields = tail_fields[part]
        two = pl.ds(2 if next_slab else 0, 2)
        slot = 2 * part + (1 if next_slab else 0)
        return pltpu.make_async_remote_copy(
            src_ref=pack.at[fields, two],
            dst_ref=tail.at[fields, two],
            send_sem=tail_send.at[slot],
            recv_sem=tail_recv.at[slot],
            device_id=(lax.max(ax - 1, 0) if next_slab else ax, middle),
            device_id_type=MESH,
        )

    def tail_start(part):
        first, count = ((0, 2), (2, FIELDS - 2))[part]

        def send(next_slab, sources):
            for f in range(first, first + count):
                for k, p in sources:
                    pack[f, k] = old[f, p, row(ROWS - 1), :]
            tail_copy(part, next_slab).start()

        @pl.when(below_middle & far_slab)
        def _():
            send(False, ((0, planes - 1), (1, planes)))

        @pl.when(below_middle & after_far)
        def _():
            send(True, ((2, 1), (3, 2)))

    def tail_end():
        for next_slab, here in ((False, far_slab), (True, after_far)):
            @pl.when(below_middle & here)
            def _():
                for part in range(2):
                    tail_copy(part, next_slab).wait_send()

    def tail_rows(part):
        first, count = ((0, 2), (2, FIELDS - 2))[part]

        @pl.when(above_middle & far_slab)
        def _():
            tail_copy(part, True).wait_recv()
            tail_copy(part, False).wait_recv()
            for k in range(2):
                w = weights(planes - 2 + k)
                for f in range(first, first + count):
                    rem[f, planes - 1 + k, 0] = (
                        w[0] * tail[f, k] + w[1] * tail[f, k + 1] + w[2] * tail[f, k + 2]
                    )

    def middle_start(group):
        @pl.when(below_middle & goes_round(group))
        def _():
            to_relay(group, False).start()

        @pl.when(above_middle)
        def _():
            to_relay(group, True).start()

    def xs_start(group, span):
        @pl.when(has_low & ~above_middle)
        def _():
            xs_copy(group, span, True).start()

        relayed = group in RELAYED and span == 0

        elsewhere = goes_round(group) if relayed else far_slab

        @pl.when(has_high & ~(below_middle & elsewhere) if relayed or span == 1 else has_high)
        def _():
            xs_copy(group, span, False).start()

    def late_start():
        @pl.when(above_middle)
        def _():
            pl.semaphore_wait(known.at[4], 1)
            for group in range(5):
                for span in range(2):
                    if span == 1 or group not in RELAYED:
                        xs_copy(group, span, True).start()

    def pass_on(group, going_down):
        @pl.when((xs == (0 if going_down else n_xs - 1)) & (going_down | goes_round(group)))
        def _():
            if going_down and group == RELAYED[0]:
                pl.semaphore_wait(known.at[4], 1)
            to_relay(group, going_down).wait_recv()
            from_relay(group, going_down).start()

    def pass_end(going_down):
        for group in RELAYED:
            @pl.when((xs == (0 if going_down else n_xs - 1)) & (going_down | goes_round(group)))
            def _():
                from_relay(group, going_down).wait_send()

    smalls[0].wait()
    loads[0].wait()
    loads[1].wait()
    remap(0, 2, 0, planes - 2)
    greeted = greeters(1) + has_high.astype(jnp.int32) + (has_low & ~above_middle).astype(jnp.int32)
    pl.semaphore_wait(
        barrier,
        greeted
        + 2 * below_middle.astype(jnp.int32)
        + above_middle.astype(jnp.int32)
        + (below_middle & after_far).astype(jnp.int32),
    )
    xs_start(0, 0)
    each_down(range(2), True, lambda c: c.start())
    tail_start(0)
    each_down(range(2, 6), True, lambda c: c.start())

    @pl.when(below_middle)
    def _():
        signal_xs(known.at[4], middle)
        signal_xs(known.at[4], 0)

    loads[2].wait()
    remap(2, 4, 0, planes - 2)
    xs_start(1, 0)
    loads[3].wait()
    remap(6, 4, 0, planes - 2)
    middle_start(3)
    middle_start(4)
    tail_start(1)
    each_up(range(4), True, lambda c: c.start())
    greet(known.at[0], 1)
    for small in smalls[1:]:
        small.wait()
    loads[4].wait()
    loads[5].wait()

    for s in range(SPECIES):
        for r in range(SPECIES):
            mix[s * SPECIES + r] = coeff_s[s, r] * rate_s[r]
    for r in range(SPECIES):
        mix[SPECIES * SPECIES + r] = heat_s[r] * rate_s[r]

    lane = lax.broadcasted_iota(jnp.int32, (CHUNKS, LANES), 1)
    chunk = lax.broadcasted_iota(jnp.int32, (CHUNKS, LANES), 0)
    at_last = lane == LANES - 1
    at_first = lane == 0
    z_end = at_last & (chunk == CHUNKS - 1)
    z_begin = at_first & (chunk == 0)

    def out_ref(i):
        f = ORDER[i]
        return temp_out if f == SPECIES else conc_out.at[f]

    def plane(q, fields=range(FIELDS)):
        for r in range(ROWS):
            for d in range(3):
                v = 0.1 * vel_v[d, q, row(r), :]
                above = 0.1 - v
                below = 0.1 + v
                if d == 2:
                    above = jnp.where(z_end, 0.0, above)
                    below = jnp.where(z_begin, 0.0, below)
                if d == 1 and r == 0:
                    edge[q, 0] = below
                if d == 1 and r == ROWS - 1:
                    edge[q, 1] = above
                coef[2 * d, r] = above
                coef[2 * d + 1, r] = below
            gas[q, r] = 0.5 * (1 - gap_v[q, row(r), :]).astype(jnp.float32)
        rates = []
        for r in range(ROWS):
            inv = -1.0 / rem[0, q + 1, r + 1]
            ys = [rem[PLACE[s], q + 1, r + 1] for s in range(SPECIES)]
            rates.append(
                [
                    jnp.exp(thresh_s[s] * inv) * (ys[s] * ys[(s + 1) % SPECIES])
                    for s in range(SPECIES)
                ]
            )
        for i in fields:
            f = ORDER[i]
            source = [None] * ROWS
            for s in range(SPECIES):
                m = mix[f * SPECIES + s]
                for r in range(ROWS):
                    term = m * rates[r][s]
                    source[r] = term if source[r] is None else source[r] + term
            mine = [rem[i, q + 1, r + 1] for r in range(ROWS)]
            for r in range(ROWS):
                x = mine[r]
                to_up = pltpu.roll(x, LANES - 1, 1)
                to_up = jnp.where(at_last, pltpu.roll(to_up, CHUNKS - 1, 0), to_up)
                to_low = pltpu.roll(x, 1, 1)
                to_low = jnp.where(at_first, pltpu.roll(to_low, 1, 0), to_low)
                total = 0.4 * x + gas[q, r] * source[r]
                total += coef[0, r] * rem[i, q + 2, r + 1] + coef[1, r] * rem[i, q, r + 1]
                total += coef[4, r] * to_up + coef[5, r] * to_low
                if r > 0:
                    total += coef[3, r] * mine[r - 1]
                if r < ROWS - 1:
                    total += coef[2, r] * mine[r + 1]
                out_ref(i)[q, row(r), :] = total

    def run_planes(first, count):
        def body(i, carry):
            plane(first + i)
            return carry

        lax.fori_loop(0, count, body, 0)

    run_planes(1, 2)
    each_down(range(2), False, lambda c: c.wait_recv())
    remap(0, 2, planes - 2, 3)
    xs_start(0, 1)
    for group in range(2, 5):
        xs_start(group, 0)
    pl.semaphore_wait(known.at[0], greeters(1))
    greet(known.at[1], 2)
    pass_on(3, False)
    run_planes(3, planes - 6)
    pl.semaphore_wait(known.at[1], greeters(2))
    greet(known.at[2], 4)
    pass_on(4, False)
    each_down(range(2, 4), False, lambda c: c.wait_recv())
    remap(2, 8, planes - 2, 2)
    for group in range(1, 5):
        xs_start(group, 1)
    pl.semaphore_wait(known.at[2], greeters(4))
    greet(known.at[3], 8)
    each_up(range(4), False, lambda c: c.wait_recv())
    remap_low(0, FIELDS)
    run_planes(0, 1)
    run_planes(planes - 3, 2)
    plane(planes - 1, range(2))
    late_start()

    def add_rows(group):
        f0, fn = GROUPS[group]

        def side(is_low):
            r = 0 if is_low else ROWS - 1
            halo = 0 if is_low else ROWS + 1

            def body(q, carry):
                c = edge[q, 0 if is_low else 1]
                for i in range(f0, f0 + fn):
                    ref = out_ref(i)
                    ref[q, row(r), :] = ref[q, row(r), :] + c * rem[i, q + 1, halo]
                return carry

            xs_copy(group, 0, not is_low).wait_recv()
            if is_low:
                @pl.when(~(above_middle & far_slab))
                def _():
                    xs_copy(group, 1, False).wait_recv()
            else:
                xs_copy(group, 1, True).wait_recv()
            lax.fori_loop(0, planes, body, 0)

        @pl.when(xs > 0)
        def _():
            side(True)

        @pl.when(xs < n_xs - 1)
        def _():
            side(False)

    tail_rows(0)
    add_rows(0)

    def glow(q, sums):
        return tuple(
            sums[r]
            + gas[q, r] * out_ref(1)[q, row(r), :] * out_ref(0)[q, row(r), :]
            for r in range(ROWS)
        )

    zero = jnp.zeros((CHUNKS, LANES), jnp.float32)
    sums = lax.fori_loop(0, planes, glow, (zero,) * ROWS)
    for r in range(ROWS):
        img[pl.ds(r, CHUNKS, stride=CHUNKS), :] = sums[r]

    def img_copy(d):
        peer = lax.rem(ax + d, n_ax)
        tile = pl.ds(pl.multiple_of((peer // 2) * CHUNKS, CHUNKS), CHUNKS)
        return pltpu.make_async_remote_copy(
            src_ref=img.at[tile],
            dst_ref=img_in.at[d - 1],
            send_sem=img_send.at[d - 1],
            recv_sem=img_recv.at[d - 1],
            device_id=(peer, xs),
            device_id_type=MESH,
        )

    pl.semaphore_wait(known.at[3], greeters(8))
    for d in sorted(range(1, n_ax), key=lambda d: abs(d - n_ax // 2)):
        img_copy(d).start()

    each_down(range(4, 6), False, lambda c: c.wait_recv())
    remap(2, 8, planes, 1)
    plane(planes - 1, range(2, FIELDS))
    tail_rows(1)
    for group in RELAYED:
        pass_on(group, True)
    for group in range(1, 5):
        add_rows(group)

    mine = img[pl.ds(pl.multiple_of((ax // 2) * CHUNKS, CHUNKS), CHUNKS), :]
    for d in range(1, n_ax):
        img_copy(d).wait_recv()
        mine = mine + img_in[d - 1]
    half = LANES // 2
    mine = jnp.where(lax.rem(ax, 2) == 1, pltpu.roll(mine, half, 1), mine)
    image_out[...] = mine[:ROWS, :half] * (2.0 / total_planes) - picture_v[...]

    for d in range(1, n_ax):
        img_copy(d).wait_send()
    each_down(range(6), True, lambda c: c.wait_send())
    each_up(range(4), True, lambda c: c.wait_send())
    tail_end()
    pass_end(False)
    pass_end(True)
    for group in range(5):
        for span in range(2):
            @pl.when(has_low)
            def _():
                xs_copy(group, span, True).wait_send()

            @pl.when(has_high & ~(below_middle & far_slab) if span == 1 else has_high)
            def _():
                xs_copy(group, span, False).wait_send()


def write_out(c, t, image, c_out, t_out, image_out, sem):
    copies = [
        pltpu.make_async_copy(c.at[pl.ds(3 * i, 3)], c_out.at[pl.ds(3 * i, 3)], sem.at[i])
        for i in range(3)
    ]
    copies.append(pltpu.make_async_copy(t, t_out, sem.at[3]))
    copies.append(pltpu.make_async_copy(image, image_out, sem.at[4]))
    for copy in copies:
        copy.start()
    for copy in copies:
        copy.wait()


def tiled(x):
    *lead, rows, width = x.shape
    x = x.reshape(*lead, rows, width // LANES, LANES)
    return jnp.swapaxes(x, -3, -2).reshape(*lead, rows * (width // LANES), LANES)


def untiled(x, rows):
    *lead, both, lanes = x.shape
    x = x.reshape(*lead, both // rows, rows, lanes)
    return jnp.swapaxes(x, -3, -2).reshape(*lead, rows, (both // rows) * lanes)


def solution(mesh):
    n_ax, n_xs = mesh.shape["ax"], mesh.shape["xs"]

    def per_device(conc, temp, vel, gap, dest, rate_k, thresh, coeff, heat, picture):
        planes = conc.shape[1]
        total_planes = planes * n_ax
        f32 = jnp.float32
        any_space = pl.BlockSpec(memory_space=pltpu.HBM)
        vmem = pl.BlockSpec(memory_space=pltpu.VMEM)
        dma = pltpu.SemaphoreType.DMA
        both = ROWS * CHUNKS
        c, t, image = pl.pallas_call(
            functools.partial(per_device_kernel, n_ax, n_xs, planes, total_planes),
            out_shape=(
                jax.ShapeDtypeStruct((SPECIES, planes, both, LANES), f32),
                jax.ShapeDtypeStruct((planes, both, LANES), f32),
                jax.ShapeDtypeStruct(picture.shape, f32),
            ),
            in_specs=[any_space] * 10,
            out_specs=(vmem, vmem, vmem),
            scratch_shapes=[
                pltpu.VMEM((FIELDS, planes + 4, both, LANES), f32),
                pltpu.VMEM((FIELDS, planes + 2, ROWS + 2, CHUNKS, LANES), f32),
                pltpu.VMEM((4, planes - 2, CHUNKS, LANES), f32),
                pltpu.VMEM((FIELDS, 4, CHUNKS, LANES), f32),
                pltpu.VMEM((FIELDS, 4, CHUNKS, LANES), f32),
                pltpu.VMEM((3, planes, both, LANES), f32),
                pltpu.VMEM((planes, both, LANES), jnp.int32),
                pltpu.VMEM((6, ROWS, CHUNKS, LANES), f32),
                pltpu.VMEM((planes, 2, CHUNKS, LANES), f32),
                pltpu.VMEM((planes, ROWS, CHUNKS, LANES), f32),
                pltpu.SMEM((FIELDS * SPECIES,), f32),
                pltpu.VMEM((CHUNKS * CHUNKS, LANES), f32),
                pltpu.VMEM((n_ax - 1, CHUNKS, LANES), f32),
                dma((6,)),
                dma((6,)),
                dma((10,)),
                dma((10,)),
                dma((20,)),
                dma((20,)),
                dma((2,)),
                dma((2,)),
                dma((4,)),
                dma((4,)),
                dma((n_ax - 1,)),
                dma((n_ax - 1,)),
                pltpu.SemaphoreType.REGULAR((5,)),
                pltpu.SMEM(dest.shape, jnp.int32),
                pltpu.SMEM(rate_k.shape, f32),
                pltpu.SMEM(thresh.shape, f32),
                pltpu.SMEM(coeff.shape, f32),
                pltpu.SMEM(heat.shape, f32),
                pltpu.VMEM(picture.shape, f32),
            ],
            compiler_params=pltpu.CompilerParams(
                collective_id=0, has_side_effects=True, vmem_limit_bytes=24 * 1024 * 1024
            ),
            name="fused_step",
        )(
            *(
                pltpu.with_memory_space_constraint(x, pltpu.HBM)
                for x in (
                    tiled(conc), tiled(temp), tiled(vel), tiled(gap),
                    dest, rate_k, thresh, coeff, heat, picture,
                )
            )
        )
        either = pl.BlockSpec(memory_space=pl.ANY)
        c, t, image = pl.pallas_call(
            write_out,
            out_shape=tuple(jax.ShapeDtypeStruct(x.shape, f32) for x in (c, t, image)),
            in_specs=[either] * 3,
            out_specs=(either,) * 3,
            scratch_shapes=[dma((5,))],
            compiler_params=pltpu.CompilerParams(vmem_limit_bytes=4 * 1024 * 1024),
            name="write_out",
        )(*(pltpu.with_memory_space_constraint(x, pltpu.VMEM) for x in (c, t, image)))
        return untiled(c, ROWS), untiled(t, ROWS), image

    in_specs = (
        P(None, "ax", "xs", None),
        P("ax", "xs", None),
        P(None, "ax", "xs", None),
        P("ax", "xs", None),
        P(),
        P(),
        P(),
        P(),
        P(),
        P("xs", "ax"),
    )
    out_specs = (P(None, "ax", "xs", None), P("ax", "xs", None), P("xs", "ax"))
    return jax.shard_map(
        per_device, mesh=mesh, in_specs=in_specs, out_specs=out_specs, check_vma=False
    )
```
